256 devices in a mesh: wide: 64 (over y, z, x_hi), narrow: 4 (over x_lo, core).
Axes of the slice: x: 4 (x_hi: 2, x_lo: 2; x = x_hi * 2 + x_lo), y: 4, z: 8, core: 2. Of those that a mesh axis runs over, the one named last changes fastest.
Arguments:
- phase: float32 [512, 256, 512], P('wide', 'narrow'), may hold values from -6 to 6
- velocity: float32 [512, 256, 512], P('wide', 'narrow'), may hold values from -6 to 6
- basis: float32 [512, 512], replicated, may hold values from -0.25 to 0.25
- dual_basis: float32 [512, 512], replicated, may hold values from -0.25 to 0.25
- wall_slope: float32 [512, 512], replicated, may hold values from -0.25 to 0.25
- decay_rates: float32 [512], replicated, may hold values from 0.25 to 4
Outputs:
- new_phase: float32 [512, 256, 512], P('wide', 'narrow')
- new_velocity: float32 [512, 256, 512], P('wide', 'narrow')
The draws below stay inside these ranges and needn't reach their ends.
All inputs are finite; a program needn't handle non-finite values.
Results may differ from the reference program's by a relative error of at most 0.00005.
Values sent between devices are 32-bit elements; how exact they have to be, the bound alone decides.
No kernel may reach another device: no remote copies, remote signals or barrier semaphores. Data moves between devices by JAX's collectives and lax.ppermute only.
A program may use at most 128 MiB of HBM per device.

```python
import math
import jax
import jax.numpy as jnp
from jax import lax

X = 512
Z = 256
Y = 512


def levels(stream_key, shape, pieces, low, largest):
    loudness, own = 1.0, jax.random.fold_in(stream_key, 6)
    for axis_at, blocks in pieces:
        heights = jnp.exp(jax.random.uniform(jax.random.fold_in(own, axis_at), (blocks,), jnp.float32, low / len(pieces), largest / len(pieces)))
        loudness = loudness * jnp.repeat(heights, shape[axis_at] // blocks).reshape([-1 if axis == axis_at else 1 for axis in range(len(shape))])
    return loudness


def bell_draw(key, extent, width, reach, cuts=(), held_as=jnp.bfloat16):
    entries = jax.random.normal(key, extent, jnp.float32) * width
    if len(cuts) > 0:
        entries = levels(key, extent, cuts, -0.22, 0.18) * entries
    return jnp.clip(entries, min=-reach, max=reach).astype(held_as)


def setup_inputs(seed: int = 0) -> dict:
    streams_of = jax.random.split(jax.random.key(seed), 7)
    phase = bell_draw(streams_of[0], (X, Z, Y), 0.5, 6.0, ((0, 64), (1, 4)), jnp.float32)
    velocity = bell_draw(streams_of[1], (X, Z, Y), 1.0, 6.0, ((0, 64), (1, 4)), jnp.float32)
    basis = bell_draw(streams_of[2], (Y, Y), Y ** -0.5, 0.25, (), jnp.float32)
    dual_basis = bell_draw(streams_of[3], (Y, Y), Y ** -0.5, 0.25, (), jnp.float32)
    wall_slope = bell_draw(streams_of[4], (Y, Y), Y ** -0.5, 0.25, (), jnp.float32)
    decay_rates = jnp.clip(jnp.exp(jax.random.uniform(streams_of[5], (Y,), jnp.float32, math.log(0.25), math.log(4.0))), 0.25, 4.0)
    return dict(phase=phase, velocity=velocity, basis=basis, dual_basis=dual_basis, wall_slope=wall_slope, decay_rates=decay_rates)


highest = lax.Precision.HIGHEST
time_step = 0.1
mobility = 0.5
stabilize = 1.0
interface_sq = 0.25
capillary = 0.5
viscosity = 0.3

def wavenumber(length):
    indices = jnp.arange(length, dtype=jnp.int32)
    signed = jnp.where(indices < length // 2, indices, indices - length)
    return signed.astype(jnp.float32) * (2.0 / length)

def tables(length):
    indices = jnp.arange(length, dtype=jnp.int32)
    product = indices[:, None] * indices[None, :] % length
    angles = product.astype(jnp.float32) * (2.0 * math.pi / length)
    scaling = 1.0 / math.sqrt(length)
    cas_table = (jnp.cos(angles) + jnp.sin(angles)) * scaling
    slope_table = wavenumber(length)[None, :] * (jnp.cos(angles) - jnp.sin(angles)) * scaling
    return (cas_table, slope_table)

def along_x(matrix, field):
    return jnp.einsum('ij,jzy->izy', matrix, field, precision=highest)

def along_z(matrix, field):
    return jnp.einsum('ij,xjy->xiy', matrix, field, precision=highest)

def along_y(matrix, field):
    return jnp.einsum('ij,xzj->xzi', matrix, field, precision=highest)

def reference(phase, velocity, basis, dual_basis, wall_slope, decay_rates):
    cas_x, slope_x = tables(X)
    cas_z, slope_z = tables(Z)
    wave_sq = wavenumber(X)[:, None, None] ** 2 + wavenumber(Z)[None, :, None] ** 2
    operator_eig = -(decay_rates[None, None, :] + wave_sq)
    phase_eig = along_y(dual_basis, phase)
    rise = along_y(wall_slope, phase)
    curvature = along_y(basis, operator_eig * phase_eig)
    span_phase = along_z(cas_z, phase)
    phys_phase = along_x(cas_x, span_phase)
    grad_x = along_x(slope_x, span_phase)
    grad_z = along_x(cas_x, along_z(slope_z, phase))
    grad_y = along_x(cas_x, along_z(cas_z, rise))
    laplace = along_x(cas_x, along_z(cas_z, curvature))
    cubed = phys_phase ** 3
    potential = cubed - phys_phase - interface_sq * laplace
    explicit = cubed - (1.0 + stabilize) * phys_phase
    force_x = capillary * potential * grad_x
    force_y = capillary * potential * grad_y
    force_z = capillary * potential * grad_z
    explicit_hat = along_z(cas_z, along_x(cas_x, explicit))
    force_hat = along_z(cas_z, along_x(cas_x, force_y))
    divergence = along_z(cas_z, along_x(-slope_x.T, force_x)) + along_z(-slope_z.T, along_x(cas_x, force_z))
    forcing = -wave_sq * force_hat - along_y(wall_slope, divergence)
    explicit_eig = along_y(dual_basis, explicit_hat)
    forcing_eig = along_y(dual_basis, forcing)
    velocity_eig = along_y(dual_basis, velocity)
    damping = 1.0 + time_step * mobility * -operator_eig * (stabilize + interface_sq * -operator_eig)
    new_phase = along_y(basis, (phase_eig + time_step * mobility * operator_eig * explicit_eig) / damping)
    new_velocity = along_y(basis, (operator_eig * velocity_eig + time_step * forcing_eig) / (operator_eig * (1.0 - time_step * viscosity * operator_eig)))
    return (new_phase, new_velocity)
```

```python
import math

import jax
import jax.numpy as jnp
import ml_dtypes
import numpy as np
from jax import lax
from jax.experimental import pallas as pl
from jax.experimental.pallas import tpu as pltpu
from jax.sharding import PartitionSpec as P

time_step = 0.1
mobility = 0.5
stabilize = 1.0
interface_sq = 0.25
capillary = 0.5
viscosity = 0.3

f32 = jnp.float32
bf16 = jnp.bfloat16
both = ("wide", "narrow")


def wavenumber(length):
    indices = np.arange(length)
    return np.where(indices < length // 2, indices, indices - length) * (2.0 / length)


def tables(length):
    indices = np.arange(length)
    angles = (indices[:, None] * indices[None, :] % length) * (2.0 * math.pi / length)
    scaling = 1.0 / math.sqrt(length)
    cas_table = (np.cos(angles) + np.sin(angles)) * scaling
    slope_table = wavenumber(length)[None, :] * (np.cos(angles) - np.sin(angles)) * scaling
    return cas_table, slope_table


def halves(table):
    high = table.astype(np.float32).astype(ml_dtypes.bfloat16)
    low = (table - high.astype(np.float64)).astype(np.float32).astype(ml_dtypes.bfloat16)
    return np.stack([high, low])


def span_tables(length, parts):
    cas, slope = tables(length)
    piece = length // parts

    def inward(table):
        out = np.zeros((parts, 2, piece, 2, length))
        for parity in range(2):
            out[:, parity, :, parity, :] = table.T.reshape(parts, piece, length)
        return halves(out.reshape(2 * length, 2 * length))

    def outward(table):
        out = np.zeros((2, length, parts, 2, piece))
        for parity in range(2):
            out[parity, :, :, parity, :] = table.T.reshape(length, parts, piece)
        return halves(out.reshape(2 * length, 2 * length))

    return inward(cas), inward(slope), outward(cas), outward(-slope.T)


def stream_tables(length):
    cas, slope = tables(length)
    half = length // 2
    ahead = [table[:half, parity::2] for table in (cas, slope) for parity in range(2)]
    back = [table[parity::2, :half] for table in (cas, -slope.T) for parity in range(2)]
    return np.stack([halves(t) for t in ahead + back])


def split(value):
    high = value.astype(bf16)
    return high, (value - high.astype(f32)).astype(bf16)


def dot3(left, right):
    def dot(a, b):
        return jnp.dot(a, b, preferred_element_type=f32)

    return dot(left[0], right[0]) + (dot(left[0], right[1]) + dot(left[1], right[0]))


def eigen_kernel(phase_ref, dual_ref, slope_ref, basis_ref, decay_ref, wave_ref, send_ref, eig_ref):
    dual = split(dual_ref[...])
    slope = split(slope_ref[...])
    basis = split(basis_ref[...])
    levels = phase_ref.shape[1]
    half = levels // 2
    width = 256

    def put(field, column, value):
        for block in range(width // 128):
            for level in range(2):
                row = field * 8 + (column // 128 + block) * 2 + level
                send_ref[pl.ds(row, half, stride=24), :] = value[
                    level * half : (level + 1) * half, block * 128 : (block + 1) * 128
                ]

    for column in range(0, phase_ref.shape[0], width):
        turned = phase_ref[column : column + width, :].T
        put(0, column, turned)
        pair = split(turned)
        eig = dot3(dual, pair)
        eig_ref[:, column : column + width] = eig
        put(1, column, dot3(slope, pair))
        operator = -(decay_ref[...] + wave_ref[:, column : column + width])
        put(2, column, dot3(basis, split(operator * eig)))


def velocity_kernel(velocity_ref, dual_ref, eig_ref):
    dual = split(dual_ref[...])
    width = 256
    for column in range(0, velocity_ref.shape[0], width):
        eig_ref[:, column : column + width] = dot3(dual, split(velocity_ref[column : column + width, :].T))


def plane_kernel(recv_ref, in_cas_ref, in_slope_ref, out_cas_ref, out_slope_ref, stream_ref, send_ref, span, hat):
    wide, narrow = recv_ref.shape[:2]
    rows = wide * 8
    step = 256
    chunk = step // 8
    blocks = span.shape[1]

    def pair(ref):
        return ref[0], ref[1]

    def spanwise(at, carry):
        here = pl.ds(at * chunk, chunk)
        target = pl.ds(pl.multiple_of(at * step, step), step)

        def load(field):
            return split(
                jnp.concatenate(
                    [recv_ref[here, n, field * 8 : field * 8 + 8, :].reshape(step, 128) for n in range(narrow)], axis=1
                )
            )

        def keep(field, value):
            for block in range(blocks):
                span[field, block, target, :] = value[:, block * 128 : (block + 1) * 128]

        phase = load(0)
        keep(0, dot3(phase, pair(in_cas_ref)))
        keep(1, dot3(phase, pair(in_slope_ref)))
        keep(2, dot3(load(1), pair(in_cas_ref)))
        keep(3, dot3(load(2), pair(in_cas_ref)))
        return carry

    lax.fori_loop(0, rows // step, spanwise, 0)

    half = rows // 2

    for level in range(2):
        own = pl.ds(level, half, stride=2)

        def ahead(field, *which):
            even, odd = (
                split(
                    jnp.concatenate(
                        [span[field, parity * (blocks // 2) + block, own, :] for block in range(blocks // 2)], axis=1
                    )
                )
                for parity in range(2)
            )
            out = []
            for at in which:
                first = dot3(pair(stream_ref.at[2 * at]), even)
                second = dot3(pair(stream_ref.at[2 * at + 1]), odd)
                out.append((first + second, first - second))
            return out

        value, grad_x = ahead(0, 0, 1)
        (grad_z,) = ahead(1, 0)
        (grad_y,) = ahead(2, 0)
        (lap,) = ahead(3, 0)
        explicit, force_x, force_y, force_z = [], [], [], []
        for part in range(2):
            v = value[part]
            cubed = v * v * v
            push = capillary * (cubed - v - interface_sq * lap[part])
            explicit.append(cubed - (1.0 + stabilize) * v)
            force_x.append(push * grad_x[part])
            force_y.append(push * grad_y[part])
            force_z.append(push * grad_z[part])

        def back(field, value, at):
            for parity, folded in enumerate((value[0] + value[1], value[0] - value[1])):
                modes = dot3(pair(stream_ref.at[4 + 2 * at + parity]), split(folded))
                for block in range(blocks // 2):
                    hat[field, parity * (blocks // 2) + block, own, :] = modes[:, block * 128 : (block + 1) * 128]

        back(0, explicit, 0)
        back(1, force_y, 0)
        back(2, force_x, 1)
        back(3, force_z, 0)

    def outward(at, carry):
        here = pl.ds(at * chunk, chunk)
        source = pl.ds(pl.multiple_of(at * step, step), step)

        def put(field, value):
            for n in range(narrow):
                send_ref[here, n, field * 8 : field * 8 + 8, :] = value[:, n * 128 : (n + 1) * 128].reshape(chunk, 8, 128)

        def load(field):
            return split(jnp.concatenate([hat[field, block, source, :] for block in range(blocks)], axis=1))

        put(0, dot3(load(0), pair(out_cas_ref)))
        put(1, dot3(load(1), pair(out_cas_ref)))
        put(2, dot3(load(2), pair(out_cas_ref)) + dot3(load(3), pair(out_slope_ref)))
        return carry

    lax.fori_loop(0, rows // step, outward, 0)


def update_kernel(
    recv_ref, eig_ref, velocity_ref, dual_ref, slope_ref, basis_ref, decay_ref, wave_ref, phase_out, velocity_out
):
    dual = split(dual_ref[...])
    slope = split(slope_ref[...])
    basis = split(basis_ref[...])
    half = eig_ref.shape[0] // 2
    width = 256

    for column in range(0, eig_ref.shape[1], width):

        def get(field):
            return jnp.concatenate(
                [
                    jnp.concatenate(
                        [
                            recv_ref[pl.ds(field * 8 + (column // 128 + block) * 2 + level, half, stride=24), :]
                            for block in range(width // 128)
                        ],
                        axis=1,
                    )
                    for level in range(2)
                ],
                axis=0,
            )

        wave = wave_ref[:, column : column + width]
        operator = -(decay_ref[...] + wave)
        explicit = dot3(dual, split(get(0)))
        damping = 1.0 + time_step * mobility * -operator * (stabilize + interface_sq * -operator)
        phase = (eig_ref[:, column : column + width] + time_step * mobility * operator * explicit) / damping
        phase_out[column : column + width, :] = dot3(basis, split(phase)).T
        forcing = -wave * get(1) - dot3(slope, split(get(2)))
        forcing = dot3(dual, split(forcing))
        velocity = (operator * velocity_ref[:, column : column + width] + time_step * forcing) / (
            operator * (1.0 - time_step * viscosity * operator)
        )
        velocity_out[column : column + width, :] = dot3(basis, split(velocity)).T


def call(kernel, shapes, scratch=(), flops=0):
    vmem = pl.BlockSpec(memory_space=pltpu.VMEM)

    def run(*operands):
        return pl.pallas_call(
            kernel,
            out_shape=shapes,
            in_specs=[vmem] * len(operands),
            out_specs=jax.tree.map(lambda _: vmem, shapes),
            scratch_shapes=list(scratch),
            compiler_params=pltpu.CompilerParams(vmem_limit_bytes=56 * 1024 * 1024),
            cost_estimate=pl.CostEstimate(flops=flops, bytes_accessed=4 << 20, transcendentals=0),
        )(*operands)

    return run


def body(phase, velocity, basis, dual_basis, wall_slope, decay_rates):
    rows_x, rows_z, levels = phase.shape
    wide, narrow = lax.axis_size("wide"), lax.axis_size("narrow")
    full_x, full_z = rows_x * wide, rows_z * narrow
    count = rows_x * rows_z
    devices = wide * narrow

    def own(length, axis, rows):
        table = jnp.asarray(wavenumber(length), f32)
        return lax.dynamic_slice_in_dim(table, lax.axis_index(axis) * rows, rows)

    wave = (own(full_x, "wide", rows_x)[:, None] ** 2 + own(full_z, "narrow", rows_z)[None, :] ** 2).reshape(1, count)
    decay = decay_rates.reshape(levels, 1)
    square = jax.ShapeDtypeStruct((levels, count), f32)
    flat = jax.ShapeDtypeStruct((devices * 24, 128), f32)
    planes = jax.ShapeDtypeStruct((wide, narrow, 24, 128), f32)

    send, phase_eig = call(eigen_kernel, (flat, square), flops=3 * 6 * 512**3)(
        phase.reshape(count, levels), dual_basis, wall_slope, basis, decay, wave
    )
    recv = lax.all_to_all(send.reshape(devices, 24, 128), both, split_axis=0, concat_axis=0, tiled=True)
    velocity_eig = call(velocity_kernel, square, flops=6 * 512**3)(velocity.reshape(count, levels), dual_basis)
    scratch = [pltpu.VMEM((4, full_z // 64, full_x, 128), f32)] * 2
    consts = [jnp.asarray(t) for t in span_tables(full_z, narrow)] + [jnp.asarray(stream_tables(full_x))]
    send = call(plane_kernel, planes, scratch, flops=300 * 2 * 256**3)(recv.reshape(planes.shape), *consts)
    recv = lax.all_to_all(send.reshape(devices, 24, 128), both, split_axis=0, concat_axis=0, tiled=True)
    outs = call(update_kernel, (square, square), flops=5 * 6 * 512**3)(
        recv.reshape(flat.shape), phase_eig, velocity_eig, dual_basis, wall_slope, basis, decay, wave
    )
    return tuple(out.reshape(phase.shape) for out in outs)


def solution(mesh):
    return jax.shard_map(
        body,
        mesh=mesh,
        in_specs=(P("wide", "narrow", None), P("wide", "narrow", None), P(), P(), P(), P()),
        out_specs=(P("wide", "narrow", None), P("wide", "narrow", None)),
        check_vma=False,
    )
```

```python
import functools
import math

import jax
import jax.numpy as jnp
import ml_dtypes
import numpy as np
from jax import lax
from jax.experimental import pallas as pl
from jax.experimental.pallas import tpu as pltpu
from jax.sharding import PartitionSpec as P

time_step = 0.1
mobility = 0.5
stabilize = 1.0
interface_sq = 0.25
capillary = 0.5
viscosity = 0.3

f32 = jnp.float32
bf16 = jnp.bfloat16


def wavenumber(length):
    indices = np.arange(length)
    return np.where(indices < length // 2, indices, indices - length) * (2.0 / length)


def tables(length):
    indices = np.arange(length)
    angles = (indices[:, None] * indices[None, :] % length) * (2.0 * math.pi / length)
    scaling = 1.0 / math.sqrt(length)
    cas_table = (np.cos(angles) + np.sin(angles)) * scaling
    slope_table = wavenumber(length)[None, :] * (np.cos(angles) - np.sin(angles)) * scaling
    return cas_table, slope_table


def halves(table):
    high = table.astype(np.float32).astype(ml_dtypes.bfloat16)
    low = (table - high.astype(np.float64)).astype(np.float32).astype(ml_dtypes.bfloat16)
    return np.stack([high, low])


def span_tables(length):
    cas, slope = tables(length)
    return np.stack([halves(cas.T), halves(slope.T), halves(-slope)])


def stream_tables(length, wide):
    cas, slope = tables(length)
    half = length // 2
    order = np.arange(half).reshape(wide, half // wide).T.reshape(half)
    ahead = [table[:half, parity::2][:, order] for table in (cas, slope) for parity in range(2)]
    back = [table[parity::2, :half][order] for table in (cas, -slope.T) for parity in range(2)]
    return np.stack([halves(t) for t in ahead + back])


def split(value):
    high = value.astype(bf16)
    return high, (value - high.astype(f32)).astype(bf16)


def dot3(left, right):
    def dot(a, b):
        return jnp.dot(a, b, preferred_element_type=f32)

    return dot(left[0], right[0]) + (dot(left[0], right[1]) + dot(left[1], right[0]))


def wave_squared(column, width, rows_x, rows_z, full_x, full_z):
    at = lax.broadcasted_iota(jnp.int32, (1, width), 1) + column

    def squared(first, own, length):
        index = first + own
        signed = jnp.where(index < length // 2, index, index - length)
        return (signed.astype(f32) * (2.0 / length)) ** 2

    return squared(lax.axis_index("wide") * rows_x, at // rows_z, full_x) + squared(
        lax.axis_index("narrow") * rows_z, at % rows_z, full_z
    )


def upright(decay_ref, width):
    turned = jnp.broadcast_to(decay_ref[...], (128, decay_ref.shape[1])).T
    return jnp.concatenate([turned] * (width // 128), axis=1)


def fetch(sources, targets, sems):
    copies = [pltpu.make_async_copy(s, t, sems.at[at]) for at, (s, t) in enumerate(zip(sources, targets))]
    for copy in copies:
        copy.start()
    return copies


def field_rows(ref, field):
    held = ref.at[field]
    return held.reshape(held.shape[0] * held.shape[1], held.shape[2])


def of_field(ref, field):
    return ref.at[:, field * 8 : field * 8 + 8]


def eigen_kernel(sizes, phase_in, dual_in, slope_in, basis_in, decay_in, send_out, eig_out, *scratch):
    send_ref, phase_ref, dual_ref, slope_ref, basis_ref, decay_ref, eig_ref, sems = scratch
    levels = phase_ref.shape[1]
    half = levels // 2
    width = 256
    columns = range(0, phase_ref.shape[0], width)
    first, second = (pl.ds(column, width) for column in columns)
    copies = fetch(
        [phase_in.at[first], phase_in.at[second], dual_in, slope_in, basis_in, decay_in],
        [phase_ref.at[first], phase_ref.at[second], dual_ref, slope_ref, basis_ref, decay_ref],
        sems,
    )
    done = []

    def leave(source, target):
        done.append(pltpu.make_async_copy(source, target, sems.at[6 + len(done)]))
        done[-1].start()

    def put(field, values):
        rows = field_rows(send_ref, field)
        for column, value in zip(columns, values):
            for block in range(width // 128):
                for level in range(2):
                    row = (column // 128 + block) * 2 + level
                    rows[pl.ds(row, half, stride=8), :] = value[
                        level * half : (level + 1) * half, block * 128 : (block + 1) * 128
                    ]
        leave(send_ref.at[field], of_field(send_out, field))

    turned = []
    for at, column in enumerate(columns):
        copies[at].wait()
        turned.append(phase_ref[column : column + width, :].T)
    put(0, turned)
    pairs = [split(value) for value in turned]
    copies[2].wait()
    dual = split(dual_ref[...])
    eig = [dot3(dual, pair) for pair in pairs]
    for column, value in zip(columns, eig):
        eig_ref[:, column : column + width] = value
    leave(eig_ref, eig_out)
    copies[3].wait()
    slope = split(slope_ref[...])
    put(1, [dot3(slope, pair) for pair in pairs])
    copies[4].wait()
    copies[5].wait()
    basis = split(basis_ref[...])
    decay = upright(decay_ref, width)
    put(
        2,
        [
            dot3(basis, split(-(decay + wave_squared(column, width, *sizes)) * value))
            for column, value in zip(columns, eig)
        ],
    )
    for copy in done:
        copy.wait()


def velocity_kernel(velocity_ref, dual_ref, slope_ref, basis_ref, eig_ref, pairs_ref):
    dual = split(dual_ref[...])
    width = 256
    for column in range(0, velocity_ref.shape[0], width):
        eig_ref[:, column : column + width] = dot3(dual, split(velocity_ref[column : column + width, :].T))
        slope = dot3(dual, split(slope_ref[:, column : column + width]))
        pairs_ref[1, 0, :, column : column + width], pairs_ref[1, 1, :, column : column + width] = split(-slope)
    pairs_ref[0, 0], pairs_ref[0, 1] = dual
    pairs_ref[2, 0], pairs_ref[2, 1] = split(basis_ref[...])


def plane_kernel(wide, narrow, recv_in, span_in, stream_in, send_out, recv_ref, send_ref, span_ref, stream_ref, sems):
    copies = fetch(
        [of_field(recv_in, 0), span_in, stream_in, of_field(recv_in, 1), of_field(recv_in, 2)],
        [recv_ref.at[0], span_ref, stream_ref, recv_ref.at[1], recv_ref.at[2]],
        sems,
    )
    done = []

    def arrive(level, *which):
        if level == 0:
            for at in which:
                copies[at].wait()

    def pair(ref):
        return ref[0], ref[1]

    lower = lax.broadcasted_iota(jnp.int32, (4 * wide, 128), 1) < 64

    def rows(n, block, level):
        return pl.ds(n * wide * 8 + block * 2 + level, wide, stride=8)

    def load(field, level):
        held = field_rows(recv_ref, field)
        parts = [
            jnp.concatenate([held[rows(n, block, level), :] for block in range(4)], axis=0)
            for n in range(narrow)
        ]
        turned = [pltpu.roll(part, 64, 1) for part in parts]
        even = [jnp.where(lower, parts[n], turned[n + 1]) for n in range(0, narrow, 2)]
        odd = [jnp.where(lower, turned[n], parts[n + 1]) for n in range(0, narrow, 2)]
        return split(jnp.concatenate(even, axis=1)), split(jnp.concatenate(odd, axis=1))

    def one_level(level):
        def across(field, at):
            return tuple(split(dot3(part, pair(span_ref.at[at]))) for part in field)

        def ahead(field, at):
            first = dot3(pair(stream_ref.at[2 * at]), field[0])
            second = dot3(pair(stream_ref.at[2 * at + 1]), field[1])
            return first + second, first - second

        arrive(level, 0)
        phase = load(0, level)
        arrive(level, 1, 2)
        spread = across(phase, 0)
        value, grad_x = ahead(spread, 0), ahead(spread, 1)
        grad_z = ahead(across(phase, 1), 0)
        arrive(level, 3, 4)
        grad_y = ahead(across(load(1, level), 0), 0)
        lap = ahead(across(load(2, level), 0), 0)
        explicit, force_x, force_y, force_z = [], [], [], []
        for part in range(2):
            v = value[part]
            cubed = v * v * v
            push = capillary * (cubed - v - interface_sq * lap[part])
            explicit.append(cubed - (1.0 + stabilize) * v)
            force_x.append(push * grad_x[part])
            force_y.append(push * grad_y[part])
            force_z.append(push * grad_z[part])

        def back(value, at):
            folded = value[0] + value[1], value[0] - value[1]
            return tuple(
                split(dot3(pair(stream_ref.at[4 + 2 * at + parity]), split(folded[parity]))) for parity in range(2)
            )

        def put(field, even, odd):
            held = field_rows(send_ref, field)
            for n in range(0, narrow, 2):
                here = slice(n * 64, n * 64 + 128)
                first, second = even[:, here], odd[:, here]
                for own, value in (
                    (n, jnp.where(lower, first, pltpu.roll(second, 64, 1))),
                    (n + 1, jnp.where(lower, pltpu.roll(first, 64, 1), second)),
                ):
                    for block in range(4):
                        held[rows(own, block, level), :] = value[block * wide : (block + 1) * wide]
            if level == 1:
                done.append(pltpu.make_async_copy(send_ref.at[field], of_field(send_out, field), sems.at[5 + field]))
                done[-1].start()

        put(0, *[dot3(part, pair(span_ref.at[0])) for part in back(explicit, 0)])
        put(1, *[dot3(part, pair(span_ref.at[0])) for part in back(force_y, 0)])
        put(
            2,
            *[
                dot3(a, pair(span_ref.at[0])) + dot3(b, pair(span_ref.at[2]))
                for a, b in zip(back(force_x, 1), back(force_z, 0))
            ],
        )

    for level in range(2):
        one_level(level)
    for copy in done:
        copy.wait()


def update_kernel(sizes, recv_in, eig_in, velocity_in, pairs_in, decay_in, phase_out, velocity_out, *scratch):
    recv_ref, eig_ref, velocity_ref, pairs_ref, decay_ref, phase_ref, result_ref, sems = scratch
    copies = fetch(
        [of_field(recv_in, 0), pairs_in.at[0], of_field(recv_in, 1), of_field(recv_in, 2)]
        + [pairs_in.at[1], decay_in, eig_in, velocity_in, pairs_in.at[2]],
        [recv_ref.at[0], pairs_ref.at[0], recv_ref.at[1], recv_ref.at[2]]
        + [pairs_ref.at[1], decay_ref, eig_ref, velocity_ref, pairs_ref.at[2]],
        sems,
    )
    half = eig_ref.shape[0] // 2
    width = 256
    columns = range(0, eig_ref.shape[1], width)

    def get(field, column):
        rows = field_rows(recv_ref, field)
        return jnp.concatenate(
            [
                jnp.concatenate(
                    [
                        rows[pl.ds((column // 128 + block) * 2 + level, half, stride=8), :]
                        for block in range(width // 128)
                    ],
                    axis=1,
                )
                for level in range(2)
            ],
            axis=0,
        )

    def pair(at):
        return pairs_ref[at, 0], pairs_ref[at, 1]

    explicit, forcing = [], []
    for column in columns:
        if column == 0:
            copies[0].wait()
        value = split(get(0, column))
        if column == 0:
            copies[1].wait()
        explicit.append(dot3(pair(0), value))
        wave = wave_squared(column, width, *sizes)
        if column == 0:
            for copy in copies[2:5]:
                copy.wait()
        value = split(-wave * get(1, column))
        other = split(get(2, column))
        forcing.append(dot3(pair(0), value) + dot3(pair(1), other))
    for copy in copies[5:]:
        copy.wait()
    decay = upright(decay_ref, width)
    done = []
    for at, column in enumerate(columns):
        here = slice(column, column + width)
        operator = -(decay + wave_squared(column, width, *sizes))
        damping = 1.0 + time_step * mobility * -operator * (stabilize + interface_sq * -operator)
        phase = (eig_ref[:, here] + time_step * mobility * operator * explicit[at]) / damping
        velocity = (operator * velocity_ref[:, here] + time_step * forcing[at]) / (
            operator * (1.0 - time_step * viscosity * operator)
        )
        for which, (value, ref, out) in enumerate(
            ((phase, phase_ref, phase_out), (velocity, result_ref, velocity_out))
        ):
            ref[here, :] = dot3(pair(2), split(value)).T
            done.append(pltpu.make_async_copy(ref.at[here], out.at[here], sems.at[9 + 2 * at + which]))
            done[-1].start()
    for copy in done:
        copy.wait()


hbm = pl.BlockSpec(memory_space=pltpu.HBM)
vmem = pl.BlockSpec(memory_space=pltpu.VMEM)


def call(kernel, ins, outs, shapes, scratch, flops, limit):
    return pl.pallas_call(
        kernel,
        out_shape=shapes,
        in_specs=ins,
        out_specs=outs,
        scratch_shapes=scratch,
        compiler_params=pltpu.CompilerParams(vmem_limit_bytes=limit << 20),
        cost_estimate=pl.CostEstimate(flops=flops, bytes_accessed=4 << 20, transcendentals=0),
    )


def stages(rows_x, rows_z, levels, wide, narrow):
    full_x, full_z = rows_x * wide, rows_z * narrow
    count = rows_x * rows_z
    sizes = rows_x, rows_z, full_x, full_z
    square = jax.ShapeDtypeStruct((levels, count), f32)
    flat = jax.ShapeDtypeStruct((wide * narrow, 24, 128), f32)
    buffer = pltpu.VMEM((3, wide * narrow, 8, 128), f32)
    pairs = jax.ShapeDtypeStruct((3, 2, levels, levels), bf16)
    held, line = pltpu.VMEM((levels, count), f32), pltpu.VMEM((1, levels), f32)
    sems = pltpu.SemaphoreType.DMA
    first = call(
        functools.partial(eigen_kernel, sizes),
        [hbm] * 5,
        [hbm, hbm],
        [flat, square],
        [buffer] + [held] * 4 + [line, held, sems((10,))],
        3 * 6 * 512**3,
        60,
    )
    beside = call(velocity_kernel, [vmem] * 4, [vmem] * 2, [square, pairs], [], 2 * 6 * 512**3, 24)
    span, stream = (jnp.asarray(t) for t in (span_tables(full_z), stream_tables(full_x, wide)))
    planes = call(
        functools.partial(plane_kernel, wide, narrow),
        [hbm] * 3,
        hbm,
        flat,
        [buffer, buffer, pltpu.VMEM(span.shape, bf16), pltpu.VMEM(stream.shape, bf16), sems((8,))],
        204 * 2 * 256**3,
        60,
    )
    last = call(
        functools.partial(update_kernel, sizes),
        [hbm] * 5,
        [hbm] * 2,
        [square] * 2,
        [buffer] + [held] * 2
        + [pltpu.VMEM(pairs.shape, bf16), line, held, held, sems((13,))],
        5 * 6 * 512**3,
        60,
    )
    return first, beside, lambda recv: planes(recv, span, stream), last


def body(phase, velocity, basis, dual_basis, wall_slope, decay_rates):
    rows_x, rows_z, levels = phase.shape
    wide, narrow = lax.axis_size("wide"), lax.axis_size("narrow")
    first, beside, planes, last = stages(rows_x, rows_z, levels, wide, narrow)
    decay = decay_rates.reshape(1, levels)

    def exchange(parts):
        return lax.all_to_all(parts, ("narrow", "wide"), split_axis=0, concat_axis=0, tiled=True)

    send, phase_eig = first(phase.reshape(-1, levels), dual_basis, wall_slope, basis, decay)
    velocity_eig, pairs = beside(velocity.reshape(-1, levels), dual_basis, wall_slope, basis)
    recv = exchange(send)
    recv, velocity_eig, pairs = lax.optimization_barrier((recv, velocity_eig, pairs))
    recv = exchange(planes(recv))
    outs = last(recv, phase_eig, velocity_eig, pairs, decay)
    return tuple(out.reshape(phase.shape) for out in outs)


def solution(mesh):
    return jax.shard_map(
        body,
        mesh=mesh,
        in_specs=(P("wide", "narrow", None), P("wide", "narrow", None), P(), P(), P(), P()),
        out_specs=(P("wide", "narrow", None), P("wide", "narrow", None)),
        check_vma=False,
    )
```

```python
import functools
import math

import jax
import jax.numpy as jnp
import ml_dtypes
import numpy as np
from jax import lax
from jax.experimental import pallas as pl
from jax.experimental.pallas import tpu as pltpu
from jax.sharding import PartitionSpec as P

time_step = 0.1
mobility = 0.5
stabilize = 1.0
interface_sq = 0.25
capillary = 0.5
viscosity = 0.3

f32 = jnp.float32
bf16 = jnp.bfloat16


def wavenumber(length):
    indices = np.arange(length)
    return np.where(indices < length // 2, indices, indices - length) * (2.0 / length)


def tables(length):
    indices = np.arange(length)
    angles = (indices[:, None] * indices[None, :] % length) * (2.0 * math.pi / length)
    scaling = 1.0 / math.sqrt(length)
    cas_table = (np.cos(angles) + np.sin(angles)) * scaling
    slope_table = wavenumber(length)[None, :] * (np.cos(angles) - np.sin(angles)) * scaling
    return cas_table, slope_table


def halves(table):
    high = table.astype(np.float32).astype(ml_dtypes.bfloat16)
    low = (table - high.astype(np.float64)).astype(np.float32).astype(ml_dtypes.bfloat16)
    return np.stack([high, low])


def span_tables(length):
    cas, slope = tables(length)
    return np.stack([halves(cas.T), halves(slope.T), halves(-slope)])


def stream_tables(length, wide):
    cas, slope = tables(length)
    half = length // 2
    order = np.arange(half).reshape(wide, half // wide).T.reshape(half)
    ahead = [table[:half, parity::2][:, order] for table in (cas, slope) for parity in range(2)]
    back = [table[parity::2, :half][order] for table in (cas, -slope.T) for parity in range(2)]
    return np.stack([halves(t) for t in ahead + back])


def split(value):
    high = value.astype(bf16)
    return high, (value - high.astype(f32)).astype(bf16)


def dot3(left, right):
    def dot(a, b):
        return jnp.dot(a, b, preferred_element_type=f32)

    return dot(left[0], right[0]) + (dot(left[0], right[1]) + dot(left[1], right[0]))


def wave_squared(column, width, rows_x, rows_z, full_x, full_z):
    at = lax.broadcasted_iota(jnp.int32, (1, width), 1) + column

    def squared(first, own, length):
        index = first + own
        signed = jnp.where(index < length // 2, index, index - length)
        return (signed.astype(f32) * (2.0 / length)) ** 2

    return squared(lax.axis_index("wide") * rows_x, at // rows_z, full_x) + squared(
        lax.axis_index("narrow") * rows_z, at % rows_z, full_z
    )


def upright(decay_ref, width):
    turned = jnp.broadcast_to(decay_ref[...], (128, decay_ref.shape[1])).T
    return jnp.concatenate([turned] * (width // 128), axis=1)


def fetch(sources, targets, sems):
    copies = [pltpu.make_async_copy(s, t, sems.at[at]) for at, (s, t) in enumerate(zip(sources, targets))]
    for copy in copies:
        copy.start()
    return copies


def field_rows(ref, field):
    held = ref.at[field]
    return held.reshape(held.shape[0] * held.shape[1], held.shape[2])


def flat_rows(ref):
    return ref.reshape(ref.shape[0] * ref.shape[1], ref.shape[2])


def of_field(ref, field):
    return ref.at[:, field * 8 : field * 8 + 8]


def eigen_kernel(
    sizes, phase_in, velocity_in, dual_in, slope_in, basis_in, decay_in, send_out, eig_out, velocity_out, *scratch
):
    send_ref, phase_ref, velocity_ref, dual_ref, slope_ref, basis_ref, decay_ref, eig_ref, other_ref, sems = scratch
    levels = phase_ref.shape[1]
    half = levels // 2
    width = 256
    columns = range(0, phase_ref.shape[0], width)
    first, second = (pl.ds(column, width) for column in columns)
    copies = fetch(
        [phase_in.at[first], phase_in.at[second], dual_in, slope_in, basis_in, decay_in, velocity_in],
        [phase_ref.at[first], phase_ref.at[second], dual_ref, slope_ref, basis_ref, decay_ref, velocity_ref],
        sems,
    )
    done = []

    def leave(source, target):
        done.append(pltpu.make_async_copy(source, target, sems.at[7 + len(done)]))
        done[-1].start()

    def put(field, values):
        rows = field_rows(send_ref, field)
        for column, value in zip(columns, values):
            for block in range(width // 128):
                for level in range(2):
                    row = (column // 128 + block) * 2 + level
                    rows[pl.ds(row, half, stride=8), :] = value[
                        level * half : (level + 1) * half, block * 128 : (block + 1) * 128
                    ]
        leave(send_ref.at[field], of_field(send_out, field))

    turned = []
    for at, column in enumerate(columns):
        copies[at].wait()
        turned.append(phase_ref[column : column + width, :].T)
    put(0, turned)
    pairs = [split(value) for value in turned]
    copies[2].wait()
    dual = split(dual_ref[...])
    eig = [dot3(dual, pair) for pair in pairs]
    for column, value in zip(columns, eig):
        eig_ref[:, column : column + width] = value
    leave(eig_ref, eig_out)
    copies[3].wait()
    slope = split(slope_ref[...])
    put(1, [dot3(slope, pair) for pair in pairs])
    copies[4].wait()
    copies[5].wait()
    basis = split(basis_ref[...])
    decay = upright(decay_ref, width)
    put(
        2,
        [
            dot3(basis, split(-(decay + wave_squared(column, width, *sizes)) * value))
            for column, value in zip(columns, eig)
        ],
    )
    copies[6].wait()
    for column in columns:
        here = slice(column, column + width)
        other_ref[:, here] = dot3(dual, split(velocity_ref[here, :].T))
        leave(other_ref.at[:, here], velocity_out.at[:, here])
    for copy in done:
        copy.wait()


def plane_kernel(wide, narrow, recv_ref, span_ref, stream_ref, send_ref):
    received, sent = flat_rows(recv_ref), flat_rows(send_ref)

    def pair(ref):
        return ref[0], ref[1]

    lower = lax.broadcasted_iota(jnp.int32, (4 * wide, 128), 1) < 64

    def rows(n, field, block, level):
        return pl.ds(n * wide * 24 + field * 8 + block * 2 + level, wide, stride=24)

    def load(field, level):
        parts = [
            jnp.concatenate([received[rows(n, field, block, level), :] for block in range(4)], axis=0)
            for n in range(narrow)
        ]
        turned = [pltpu.roll(part, 64, 1) for part in parts]
        even = [jnp.where(lower, parts[n], turned[n + 1]) for n in range(0, narrow, 2)]
        odd = [jnp.where(lower, turned[n], parts[n + 1]) for n in range(0, narrow, 2)]
        return split(jnp.concatenate(even, axis=1)), split(jnp.concatenate(odd, axis=1))

    def one_level(level):
        def across(field, at):
            return tuple(split(dot3(part, pair(span_ref.at[at]))) for part in field)

        def ahead(field, at):
            first = dot3(pair(stream_ref.at[2 * at]), field[0])
            second = dot3(pair(stream_ref.at[2 * at + 1]), field[1])
            return first + second, first - second

        phase = load(0, level)
        spread = across(phase, 0)
        value, grad_x = ahead(spread, 0), ahead(spread, 1)
        grad_z = ahead(across(phase, 1), 0)
        grad_y = ahead(across(load(1, level), 0), 0)
        lap = ahead(across(load(2, level), 0), 0)
        explicit, force_x, force_y, force_z = [], [], [], []
        for part in range(2):
            v = value[part]
            cubed = v * v * v
            push = capillary * (cubed - v - interface_sq * lap[part])
            explicit.append(cubed - (1.0 + stabilize) * v)
            force_x.append(push * grad_x[part])
            force_y.append(push * grad_y[part])
            force_z.append(push * grad_z[part])

        def back(value, at):
            folded = value[0] + value[1], value[0] - value[1]
            return tuple(
                split(dot3(pair(stream_ref.at[4 + 2 * at + parity]), split(folded[parity]))) for parity in range(2)
            )

        def put(field, even, odd):
            for n in range(0, narrow, 2):
                here = slice(n * 64, n * 64 + 128)
                first, second = even[:, here], odd[:, here]
                for own, value in (
                    (n, jnp.where(lower, first, pltpu.roll(second, 64, 1))),
                    (n + 1, jnp.where(lower, pltpu.roll(first, 64, 1), second)),
                ):
                    for block in range(4):
                        sent[rows(own, field, block, level), :] = value[block * wide : (block + 1) * wide]

        put(0, *[dot3(part, pair(span_ref.at[0])) for part in back(explicit, 0)])
        put(1, *[dot3(part, pair(span_ref.at[0])) for part in back(force_y, 0)])
        put(
            2,
            *[
                dot3(a, pair(span_ref.at[0])) + dot3(b, pair(span_ref.at[2]))
                for a, b in zip(back(force_x, 1), back(force_z, 0))
            ],
        )

    for level in range(2):
        one_level(level)


def update_kernel(
    sizes,
    recv_ref,
    eig_ref,
    velocity_ref,
    dual_ref,
    slope_ref,
    basis_ref,
    decay_ref,
    phase_out,
    velocity_out,
    phase_ref,
    result_ref,
    sems,
):
    half = eig_ref.shape[0] // 2
    width = 256
    columns = range(0, eig_ref.shape[1], width)

    def get(field, column):
        rows = flat_rows(recv_ref)
        return jnp.concatenate(
            [
                jnp.concatenate(
                    [
                        rows[pl.ds(field * 8 + (column // 128 + block) * 2 + level, half, stride=24), :]
                        for block in range(width // 128)
                    ],
                    axis=1,
                )
                for level in range(2)
            ],
            axis=0,
        )

    dual = split(dual_ref[...])
    slope = split(slope_ref[...])
    basis = split(basis_ref[...])
    explicit = [dot3(dual, split(get(0, column))) for column in columns]
    forcing = [
        -wave_squared(column, width, *sizes) * get(1, column) - dot3(slope, split(get(2, column)))
        for column in columns
    ]
    forcing = [dot3(dual, split(value)) for value in forcing]
    decay = upright(decay_ref, width)
    done = []
    for at, column in enumerate(columns):
        here = slice(column, column + width)
        operator = -(decay + wave_squared(column, width, *sizes))
        damping = 1.0 + time_step * mobility * -operator * (stabilize + interface_sq * -operator)
        phase = (eig_ref[:, here] + time_step * mobility * operator * explicit[at]) / damping
        velocity = (operator * velocity_ref[:, here] + time_step * forcing[at]) / (
            operator * (1.0 - time_step * viscosity * operator)
        )
        for which, (value, ref, out) in enumerate(
            ((phase, phase_ref, phase_out), (velocity, result_ref, velocity_out))
        ):
            ref[here, :] = dot3(basis, split(value)).T
            done.append(pltpu.make_async_copy(ref.at[here], out.at[here], sems.at[2 * at + which]))
            done[-1].start()
    for copy in done:
        copy.wait()


hbm = pl.BlockSpec(memory_space=pltpu.HBM)
vmem = pl.BlockSpec(memory_space=pltpu.VMEM)


def call(kernel, ins, outs, shapes, scratch, flops, limit):
    return pl.pallas_call(
        kernel,
        out_shape=shapes,
        in_specs=ins,
        out_specs=outs,
        scratch_shapes=scratch,
        compiler_params=pltpu.CompilerParams(vmem_limit_bytes=limit << 20),
        cost_estimate=pl.CostEstimate(flops=flops, bytes_accessed=4 << 20, transcendentals=0),
    )


def stages(rows_x, rows_z, levels, wide, narrow):
    full_x, full_z = rows_x * wide, rows_z * narrow
    count = rows_x * rows_z
    sizes = rows_x, rows_z, full_x, full_z
    square = jax.ShapeDtypeStruct((levels, count), f32)
    result = jax.ShapeDtypeStruct((count, levels), f32)
    parts = jax.ShapeDtypeStruct((wide * narrow, 24, 128), f32)
    buffer = pltpu.VMEM((3, wide * narrow, 8, 128), f32)
    held, line = pltpu.VMEM((levels, count), f32), pltpu.VMEM((1, levels), f32)
    sems = pltpu.SemaphoreType.DMA
    first = call(
        functools.partial(eigen_kernel, sizes),
        [hbm] * 6,
        [hbm] * 3,
        [parts, square, square],
        [buffer] + [held] * 5 + [line, held, held, sems((13,))],
        4 * 6 * 512**3,
        60,
    )
    span, stream = (jnp.asarray(t) for t in (span_tables(full_z), stream_tables(full_x, wide)))
    planes = call(
        functools.partial(plane_kernel, wide, narrow), [vmem] * 3, vmem, parts, [], 204 * 2 * 256**3, 40
    )
    last = call(
        functools.partial(update_kernel, sizes),
        [vmem] * 7,
        [hbm] * 2,
        [result] * 2,
        [held, held, sems((4,))],
        5 * 6 * 512**3,
        40,
    )
    return first, lambda recv: planes(recv, span, stream), last


def body(phase, velocity, basis, dual_basis, wall_slope, decay_rates):
    rows_x, rows_z, levels = phase.shape
    wide, narrow = lax.axis_size("wide"), lax.axis_size("narrow")
    first, planes, last = stages(rows_x, rows_z, levels, wide, narrow)
    decay = decay_rates.reshape(1, levels)

    def exchange(parts):
        return lax.all_to_all(parts, ("narrow", "wide"), split_axis=0, concat_axis=0, tiled=True)

    send, phase_eig, velocity_eig = first(
        phase.reshape(-1, levels), velocity.reshape(-1, levels), dual_basis, wall_slope, basis, decay
    )
    recv = exchange(planes(exchange(send)))
    outs = last(recv, phase_eig, velocity_eig, dual_basis, wall_slope, basis, decay)
    return tuple(out.reshape(phase.shape) for out in outs)


def solution(mesh):
    return jax.shard_map(
        body,
        mesh=mesh,
        in_specs=(P("wide", "narrow", None), P("wide", "narrow", None), P(), P(), P(), P()),
        out_specs=(P("wide", "narrow", None), P("wide", "narrow", None)),
        check_vma=False,
    )
```

```python
import functools
import math

import jax
import jax.numpy as jnp
import ml_dtypes
import numpy as np
from jax import lax
from jax.experimental import pallas as pl
from jax.experimental.pallas import tpu as pltpu
from jax.sharding import PartitionSpec as P

time_step = 0.1
mobility = 0.5
stabilize = 1.0
interface_sq = 0.25
capillary = 0.5
viscosity = 0.3

f32 = jnp.float32
bf16 = jnp.bfloat16


def wavenumber(length):
    indices = np.arange(length)
    return np.where(indices < length // 2, indices, indices - length) * (2.0 / length)


def tables(length):
    indices = np.arange(length)
    angles = (indices[:, None] * indices[None, :] % length) * (2.0 * math.pi / length)
    scaling = 1.0 / math.sqrt(length)
    cas_table = (np.cos(angles) + np.sin(angles)) * scaling
    slope_table = wavenumber(length)[None, :] * (np.cos(angles) - np.sin(angles)) * scaling
    return cas_table, slope_table


def halves(table):
    high = table.astype(np.float32).astype(ml_dtypes.bfloat16)
    low = (table - high.astype(np.float64)).astype(np.float32).astype(ml_dtypes.bfloat16)
    return np.stack([high, low])


def span_tables(length):
    cas, slope = tables(length)
    return np.stack([halves(cas.T), halves(slope.T), halves(-slope)])


def stream_tables(length, wide):
    cas, slope = tables(length)
    half = length // 2
    order = np.arange(half).reshape(wide, half // wide).T.reshape(half)
    ahead = [table[:half, parity::2][:, order] for table in (cas, slope) for parity in range(2)]
    back = [table[parity::2, :half][order] for table in (cas, -slope.T) for parity in range(2)]
    return np.stack([halves(t) for t in ahead + back])


def split(value):
    high = value.astype(bf16)
    return high, (value - high.astype(f32)).astype(bf16)


def dot3(left, right):
    def dot(a, b):
        return jnp.dot(a, b, preferred_element_type=f32)

    return dot(left[0], right[0]) + (dot(left[0], right[1]) + dot(left[1], right[0]))


def dot3_left(left, right):
    rows = left[0].shape[0]
    first = jnp.dot(jnp.concatenate([left[0], left[1]], axis=0), right[0], preferred_element_type=f32)
    return first[:rows] + first[rows:] + jnp.dot(left[0], right[1], preferred_element_type=f32)


def wave_squared(column, width, rows_x, rows_z, full_x, full_z):
    at = lax.broadcasted_iota(jnp.int32, (1, width), 1) + column

    def squared(first, own, length):
        index = first + own
        signed = jnp.where(index < length // 2, index, index - length)
        return (signed.astype(f32) * (2.0 / length)) ** 2

    return squared(lax.axis_index("wide") * rows_x, at // rows_z, full_x) + squared(
        lax.axis_index("narrow") * rows_z, at % rows_z, full_z
    )


def upright(decay_ref, width):
    turned = jnp.broadcast_to(decay_ref[...], (128, decay_ref.shape[1])).T
    return jnp.concatenate([turned] * (width // 128), axis=1)


def fetch(sources, targets, sems, early):
    copies = [pltpu.make_async_copy(s, t, sems.at[at]) for at, (s, t) in enumerate(zip(sources, targets))]
    for copy in copies[:early]:
        copy.start()
    return copies


def field_rows(ref, field):
    held = ref.at[field]
    return held.reshape(held.shape[0] * held.shape[1], held.shape[2])


def flat_rows(ref):
    return ref.reshape(ref.shape[0] * ref.shape[1], ref.shape[2])


def of_field(ref, field):
    return ref.at[:, field * 8 : field * 8 + 8]


def eigen_kernel(
    sizes, phase_in, dual_in, slope_in, basis_in, decay_in, send_out, eig_out, *scratch
):
    send_ref, phase_ref, dual_ref, slope_ref, basis_ref, decay_ref, eig_ref, sems = scratch
    levels = phase_ref.shape[1]
    half = levels // 2
    width = 256
    columns = range(0, phase_ref.shape[0], width)
    first, second = (pl.ds(column, width) for column in columns)
    copies = fetch(
        [phase_in.at[first], phase_in.at[second], dual_in, slope_in, basis_in, decay_in],
        [phase_ref.at[first], phase_ref.at[second], dual_ref, slope_ref, basis_ref, decay_ref],
        sems,
        3,
    )
    done = []

    def leave(source, target):
        done.append(pltpu.make_async_copy(source, target, sems.at[6 + len(done)]))
        done[-1].start()

    def put(field, values):
        rows = field_rows(send_ref, field)
        for column, value in zip(columns, values):
            for block in range(width // 128):
                for level in range(2):
                    row = (column // 128 + block) * 2 + level
                    rows[pl.ds(row, half, stride=8), :] = value[
                        level * half : (level + 1) * half, block * 128 : (block + 1) * 128
                    ]
        leave(send_ref.at[field], of_field(send_out, field))

    turned = []
    for at, column in enumerate(columns):
        copies[at].wait()
        if at == 0:
            for copy in copies[3:]:
                copy.start()
        turned.append(phase_ref[column : column + width, :].T)
    put(0, turned)
    pairs = [split(value) for value in turned]
    copies[2].wait()
    dual = split(dual_ref[...])
    eig = [dot3(dual, pair) for pair in pairs]
    for column, value in zip(columns, eig):
        eig_ref[:, column : column + width] = value
    leave(eig_ref, eig_out)
    copies[3].wait()
    slope = split(slope_ref[...])
    put(1, [dot3(slope, pair) for pair in pairs])
    copies[4].wait()
    copies[5].wait()
    basis = split(basis_ref[...])
    decay = upright(decay_ref, width)
    scaled = [
        split(-(decay + wave_squared(column, width, *sizes)) * value) for column, value in zip(columns, eig)
    ]
    rows = field_rows(send_ref, 2)
    part = half // 2
    for own in range(2):
        mine = [
            jnp.concatenate([b[at : at + part] for at in (own * part, half + own * part)], axis=0) for b in basis
        ]
        for column, pair in zip(columns, scaled):
            value = dot3(mine, pair)
            for block in range(width // 128):
                for level in range(2):
                    row = own * part * 8 + (column // 128 + block) * 2 + level
                    rows[pl.ds(row, part, stride=8), :] = value[
                        level * part : (level + 1) * part, block * 128 : (block + 1) * 128
                    ]
        devices = slice(own * part, (own + 1) * part)
        leave(send_ref.at[2, devices], send_out.at[devices, 16:24])
    for copy in done:
        copy.wait()


def plane_kernel(wide, narrow, recv_ref, span_ref, stream_ref, send_ref):
    received, sent = flat_rows(recv_ref), flat_rows(send_ref)

    def pair(ref):
        return ref[0], ref[1]

    lower = lax.broadcasted_iota(jnp.int32, (4 * wide, 128), 1) < 64

    def rows(n, field, block, level):
        return pl.ds(n * wide * 24 + field * 8 + block * 2 + level, wide, stride=24)

    def load(field, level):
        parts = [
            jnp.concatenate([received[rows(n, field, block, level), :] for block in range(4)], axis=0)
            for n in range(narrow)
        ]
        turned = [pltpu.roll(part, 64, 1) for part in parts]
        even = [jnp.where(lower, parts[n], turned[n + 1]) for n in range(0, narrow, 2)]
        odd = [jnp.where(lower, turned[n], parts[n + 1]) for n in range(0, narrow, 2)]
        return jnp.concatenate([jnp.concatenate(even, axis=1), jnp.concatenate(odd, axis=1)], axis=0)

    half = 4 * wide

    def across(values, at):
        return split(dot3(values, pair(span_ref.at[at])))

    def ahead(field, at):
        first = dot3_left(pair(stream_ref.at[2 * at]), tuple(f[:half] for f in field))
        second = dot3_left(pair(stream_ref.at[2 * at + 1]), tuple(f[half:] for f in field))
        return first + second, first - second

    def beside(pairs):
        return tuple(jnp.concatenate(part, axis=1) for part in zip(*pairs))

    def ahead_both(fields, at):
        first = dot3_left(pair(stream_ref.at[2 * at]), beside([tuple(f[:half] for f in field) for field in fields]))
        second = dot3_left(
            pair(stream_ref.at[2 * at + 1]), beside([tuple(f[half:] for f in field) for field in fields])
        )
        points = first.shape[1] // 2
        out = first + second, first - second
        return [[o[:, :points] for o in out], [o[:, points:] for o in out]]

    both = range(2)
    phase = [split(load(0, level)) for level in both]
    spread = [across(phase[level], 0) for level in both]
    slope = [across(phase[level], 1) for level in both]
    value = ahead_both(spread, 0)
    rise = [split(load(1, level)) for level in both]
    grad_x = ahead_both(spread, 1)
    rise = [across(rise[level], 0) for level in both]
    grad_z = ahead_both(slope, 0)
    bend = [split(load(2, level)) for level in both]
    grad_y = ahead_both(rise, 0)
    bend = [across(bend[level], 0) for level in both]
    lap = ahead_both(bend, 0)

    def back(value, at):
        folded = value[0] + value[1], value[0] - value[1]
        return split(
            jnp.concatenate(
                [dot3_left(pair(stream_ref.at[4 + 2 * at + parity]), split(folded[parity])) for parity in range(2)],
                axis=0,
            )
        )

    def put(field, level, modes):
        even, odd = modes[:half], modes[half:]
        for n in range(0, narrow, 2):
            here = slice(n * 64, n * 64 + 128)
            first, second = even[:, here], odd[:, here]
            for own, value in (
                (n, jnp.where(lower, first, pltpu.roll(second, 64, 1))),
                (n + 1, jnp.where(lower, pltpu.roll(first, 64, 1), second)),
            ):
                for block in range(4):
                    sent[rows(own, field, block, level), :] = value[block * wide : (block + 1) * wide]

    cubed = [[v * v * v for v in value[level]] for level in both]
    explicit = [
        [c - (1.0 + stabilize) * v for c, v in zip(cubed[level], value[level])] for level in both
    ]
    explicit = [back(explicit[level], 0) for level in both]
    push = [
        [capillary * (c - v - interface_sq * l) for c, v, l in zip(cubed[level], value[level], lap[level])]
        for level in both
    ]

    def force(level, slopes):
        return [p * g for p, g in zip(push[level], slopes[level])]

    along = [back(force(level, grad_y), 0) for level in both]
    for level in both:
        put(0, level, dot3(explicit[level], pair(span_ref.at[0])))
    spread = [back(force(level, grad_x), 1) for level in both]
    for level in both:
        put(1, level, dot3(along[level], pair(span_ref.at[0])))
    slope = [back(force(level, grad_z), 0) for level in both]
    for level in both:
        put(2, level, dot3(spread[level], pair(span_ref.at[0])) + dot3(slope[level], pair(span_ref.at[2])))


def update_kernel(
    sizes,
    recv_ref,
    eig_ref,
    velocity_ref,
    dual_ref,
    slope_ref,
    basis_ref,
    decay_ref,
    phase_out,
    velocity_out,
    phase_ref,
    result_ref,
    sems,
):
    half = eig_ref.shape[0] // 2
    width = 256
    columns = range(0, eig_ref.shape[1], width)

    def get(field, column):
        rows = flat_rows(recv_ref)
        return jnp.concatenate(
            [
                jnp.concatenate(
                    [
                        rows[pl.ds(field * 8 + (column // 128 + block) * 2 + level, half, stride=24), :]
                        for block in range(width // 128)
                    ],
                    axis=1,
                )
                for level in range(2)
            ],
            axis=0,
        )

    dual = split(dual_ref[...])
    slope = split(slope_ref[...])
    basis = split(basis_ref[...])
    decay = upright(decay_ref, width)
    waves = [wave_squared(column, width, *sizes) for column in columns]
    operators = [-(decay + wave) for wave in waves]
    done = []

    def leave(which, column, value):
        ref, out = ((phase_ref, phase_out), (result_ref, velocity_out))[which]
        here = slice(column, column + width)
        ref[here, :] = value
        done.append(pltpu.make_async_copy(ref.at[here], out.at[here], sems.at[len(done)]))
        done[-1].start()

    def new_phase(column, operator, explicit):
        damping = 1.0 + time_step * mobility * -operator * (stabilize + interface_sq * -operator)
        return (eig_ref[:, column : column + width] + time_step * mobility * operator * explicit) / damping

    def new_velocity(operator, speed, forcing):
        return (operator * speed + time_step * forcing) / (operator * (1.0 - time_step * viscosity * operator))

    forcing = [dot3(slope, split(get(2, column))) for column in columns]
    explicit = [dot3(dual, split(get(0, column))) for column in columns]
    forcing = [split(-wave * get(1, column) - value) for column, wave, value in zip(columns, waves, forcing)]
    forcing = [dot3(dual, value) for value in forcing]
    explicit = [split(new_phase(*at)) for at in zip(columns, operators, explicit)]
    speed = [dot3(dual, split(velocity_ref[column : column + width, :].T)) for column in columns]
    turned = split(basis_ref[...].T)
    explicit = [dot3(tuple(v.T for v in value), turned) for value in explicit]
    speed = [split(new_velocity(*at)) for at in zip(operators, speed, forcing)]
    for column, value in zip(columns, explicit):
        leave(0, column, value)
    for column, value in zip(columns, speed):
        leave(1, column, dot3(tuple(v.T for v in value), turned))
    for copy in done:
        copy.wait()


hbm = pl.BlockSpec(memory_space=pltpu.HBM)
vmem = pl.BlockSpec(memory_space=pltpu.VMEM)


def call(kernel, ins, outs, shapes, scratch, flops, limit):
    return pl.pallas_call(
        kernel,
        out_shape=shapes,
        in_specs=ins,
        out_specs=outs,
        scratch_shapes=scratch,
        compiler_params=pltpu.CompilerParams(vmem_limit_bytes=limit << 20),
        cost_estimate=pl.CostEstimate(flops=flops, bytes_accessed=4 << 20, transcendentals=0),
    )


def stages(rows_x, rows_z, levels, wide, narrow):
    full_x, full_z = rows_x * wide, rows_z * narrow
    count = rows_x * rows_z
    sizes = rows_x, rows_z, full_x, full_z
    square = jax.ShapeDtypeStruct((levels, count), f32)
    result = jax.ShapeDtypeStruct((count, levels), f32)
    parts = jax.ShapeDtypeStruct((wide * narrow, 24, 128), f32)
    buffer = pltpu.VMEM((3, wide * narrow, 8, 128), f32)
    held, line = pltpu.VMEM((levels, count), f32), pltpu.VMEM((1, levels), f32)
    sems = pltpu.SemaphoreType.DMA
    first = call(
        functools.partial(eigen_kernel, sizes),
        [hbm] * 5,
        [hbm] * 2,
        [parts, square],
        [buffer] + [held] * 4 + [line, held, sems((11,))],
        3 * 6 * 512**3,
        60,
    )
    span, stream = (jnp.asarray(t) for t in (span_tables(full_z), stream_tables(full_x, wide)))
    planes = call(
        functools.partial(plane_kernel, wide, narrow), [vmem] * 3, vmem, parts, [], 204 * 2 * 256**3, 40
    )
    last = call(
        functools.partial(update_kernel, sizes),
        [vmem] * 7,
        [hbm] * 2,
        [result] * 2,
        [held, held, sems((4,))],
        5 * 6 * 512**3,
        40,
    )
    return first, lambda recv: planes(recv, span, stream), last


def body(phase, velocity, basis, dual_basis, wall_slope, decay_rates):
    rows_x, rows_z, levels = phase.shape
    wide, narrow = lax.axis_size("wide"), lax.axis_size("narrow")
    first, planes, last = stages(rows_x, rows_z, levels, wide, narrow)
    decay = decay_rates.reshape(1, levels)

    def exchange(parts):
        return lax.all_to_all(parts, ("narrow", "wide"), split_axis=0, concat_axis=0, tiled=True)

    send, phase_eig = first(phase.reshape(-1, levels), dual_basis, wall_slope, basis, decay)
    recv = exchange(planes(exchange(send)))
    outs = last(recv, phase_eig, velocity.reshape(-1, levels), dual_basis, wall_slope, basis, decay)
    return tuple(out.reshape(phase.shape) for out in outs)


def solution(mesh):
    return jax.shard_map(
        body,
        mesh=mesh,
        in_specs=(P("wide", "narrow", None), P("wide", "narrow", None), P(), P(), P(), P()),
        out_specs=(P("wide", "narrow", None), P("wide", "narrow", None)),
        check_vma=False,
    )
```

```python
import functools
import math

import jax
import jax.numpy as jnp
import ml_dtypes
import numpy as np
from jax import lax
from jax.experimental import pallas as pl
from jax.experimental.pallas import tpu as pltpu
from jax.sharding import PartitionSpec as P

time_step = 0.1
mobility = 0.5
stabilize = 1.0
interface_sq = 0.25
capillary = 0.5
viscosity = 0.3

f32 = jnp.float32
bf16 = jnp.bfloat16


def wavenumber(length):
    indices = np.arange(length)
    return np.where(indices < length // 2, indices, indices - length) * (2.0 / length)


def tables(length):
    indices = np.arange(length)
    angles = (indices[:, None] * indices[None, :] % length) * (2.0 * math.pi / length)
    scaling = 1.0 / math.sqrt(length)
    cas_table = (np.cos(angles) + np.sin(angles)) * scaling
    slope_table = wavenumber(length)[None, :] * (np.cos(angles) - np.sin(angles)) * scaling
    return cas_table, slope_table


def halves(table):
    high = table.astype(np.float32).astype(ml_dtypes.bfloat16)
    low = (table - high.astype(np.float64)).astype(np.float32).astype(ml_dtypes.bfloat16)
    return np.stack([high, low])


def span_tables(length):
    cas, slope = tables(length)
    return np.stack([halves(cas.T), halves(slope.T), halves(-slope)])


def stream_tables(length, wide):
    cas, slope = tables(length)
    half = length // 2
    order = np.arange(half).reshape(wide, half // wide).T.reshape(half)
    ahead = [table[:half, parity::2][:, order] for table in (cas, slope) for parity in range(2)]
    back = [table[parity::2, :half][order] for table in (cas, -slope.T) for parity in range(2)]
    return np.stack([halves(t) for t in ahead + back])


def split(value):
    high = value.astype(bf16)
    return high, (value - high.astype(f32)).astype(bf16)


def dot3(left, right):
    def dot(a, b):
        return jnp.dot(a, b, preferred_element_type=f32)

    return dot(left[0], right[0]) + (dot(left[0], right[1]) + dot(left[1], right[0]))


def dot3_left(left, right):
    rows = left[0].shape[0]
    first = jnp.dot(jnp.concatenate([left[0], left[1]], axis=0), right[0], preferred_element_type=f32)
    return first[:rows] + first[rows:] + jnp.dot(left[0], right[1], preferred_element_type=f32)


def wave_squared(column, width, rows_x, rows_z, full_x, full_z):
    at = lax.broadcasted_iota(jnp.int32, (1, width), 1) + column

    def squared(first, own, length):
        index = first + own
        signed = jnp.where(index < length // 2, index, index - length)
        return (signed.astype(f32) * (2.0 / length)) ** 2

    return squared(lax.axis_index("wide") * rows_x, at // rows_z, full_x) + squared(
        lax.axis_index("narrow") * rows_z, at % rows_z, full_z
    )


def upright(decay_ref, width):
    turned = jnp.broadcast_to(decay_ref[...], (128, decay_ref.shape[1])).T
    return jnp.concatenate([turned] * (width // 128), axis=1)


def fetch(sources, targets, sems, early):
    copies = [pltpu.make_async_copy(s, t, sems.at[at]) for at, (s, t) in enumerate(zip(sources, targets))]
    for copy in copies[:early]:
        copy.start()
    return copies


def field_rows(ref, field):
    held = ref.at[field]
    return held.reshape(held.shape[0] * held.shape[1], held.shape[2])


def flat_rows(ref):
    return ref.reshape(ref.shape[0] * ref.shape[1], ref.shape[2])


def of_field(ref, field):
    return ref.at[:, field * 8 : field * 8 + 8]


def eigen_kernel(
    sizes, phase_in, dual_in, slope_in, basis_in, decay_in, send_out, eig_out, *scratch
):
    send_ref, phase_ref, dual_ref, slope_ref, basis_ref, decay_ref, eig_ref, sems = scratch
    levels = phase_ref.shape[1]
    half = levels // 2
    width = 256
    columns = range(0, phase_ref.shape[0], width)
    first, second = (pl.ds(column, width) for column in columns)
    copies = fetch(
        [phase_in.at[first], phase_in.at[second], dual_in, slope_in, basis_in, decay_in],
        [phase_ref.at[first], phase_ref.at[second], dual_ref, slope_ref, basis_ref, decay_ref],
        sems,
        4,
    )
    done = []

    def leave(source, target):
        done.append(pltpu.make_async_copy(source, target, sems.at[6 + len(done)]))
        done[-1].start()

    def put(field, values):
        rows = field_rows(send_ref, field)
        for column, value in zip(columns, values):
            for block in range(width // 128):
                for level in range(2):
                    row = (column // 128 + block) * 2 + level
                    rows[pl.ds(row, half, stride=8), :] = value[
                        level * half : (level + 1) * half, block * 128 : (block + 1) * 128
                    ]
        leave(send_ref.at[field], of_field(send_out, field))

    turned = []
    for at, column in enumerate(columns):
        copies[at].wait()
        if at == 0:
            for copy in copies[4:]:
                copy.start()
        turned.append(phase_ref[column : column + width, :].T)
    put(0, turned)
    pairs = [split(value) for value in turned]
    copies[2].wait()
    dual = split(dual_ref[...])
    eig = [dot3_left(dual, pair) for pair in pairs]
    for column, value in zip(columns, eig):
        eig_ref[:, column : column + width] = value
    leave(eig_ref, eig_out)
    copies[3].wait()
    slope = split(slope_ref[...])
    put(1, [dot3_left(slope, pair) for pair in pairs])
    copies[4].wait()
    copies[5].wait()
    basis = split(basis_ref[...])
    decay = upright(decay_ref, width)
    scaled = [
        split(-(decay + wave_squared(column, width, *sizes)) * value) for column, value in zip(columns, eig)
    ]
    rows = field_rows(send_ref, 2)
    part = half // 2
    for own in range(2):
        mine = [
            jnp.concatenate([b[at : at + part] for at in (own * part, half + own * part)], axis=0) for b in basis
        ]
        for column, pair in zip(columns, scaled):
            value = dot3_left(mine, pair)
            for block in range(width // 128):
                for level in range(2):
                    row = own * part * 8 + (column // 128 + block) * 2 + level
                    rows[pl.ds(row, part, stride=8), :] = value[
                        level * part : (level + 1) * part, block * 128 : (block + 1) * 128
                    ]
        devices = slice(own * part, (own + 1) * part)
        leave(send_ref.at[2, devices], send_out.at[devices, 16:24])
    for copy in done:
        copy.wait()


def plane_kernel(wide, narrow, recv_ref, span_ref, stream_ref, send_ref):
    received, sent = flat_rows(recv_ref), flat_rows(send_ref)

    def pair(ref):
        return ref[0], ref[1]

    lower = lax.broadcasted_iota(jnp.int32, (4 * wide, 128), 1) < 64

    def rows(n, field, block, level):
        return pl.ds(n * wide * 24 + field * 8 + block * 2 + level, wide, stride=24)

    def load(field, level):
        parts = [
            jnp.concatenate([received[rows(n, field, block, level), :] for block in range(4)], axis=0)
            for n in range(narrow)
        ]
        turned = [pltpu.roll(part, 64, 1) for part in parts]
        even = [jnp.where(lower, parts[n], turned[n + 1]) for n in range(0, narrow, 2)]
        odd = [jnp.where(lower, turned[n], parts[n + 1]) for n in range(0, narrow, 2)]
        return jnp.concatenate([jnp.concatenate(even, axis=1), jnp.concatenate(odd, axis=1)], axis=0)

    half = 4 * wide

    def across(values, at):
        return split(dot3(values, pair(span_ref.at[at])))

    def ahead(field, at):
        first = dot3_left(pair(stream_ref.at[2 * at]), tuple(f[:half] for f in field))
        second = dot3_left(pair(stream_ref.at[2 * at + 1]), tuple(f[half:] for f in field))
        return first + second, first - second

    def beside(pairs):
        return tuple(jnp.concatenate(part, axis=1) for part in zip(*pairs))

    def ahead_both(fields, at):
        first = dot3_left(pair(stream_ref.at[2 * at]), beside([tuple(f[:half] for f in field) for field in fields]))
        second = dot3_left(
            pair(stream_ref.at[2 * at + 1]), beside([tuple(f[half:] for f in field) for field in fields])
        )
        points = first.shape[1] // 2
        out = first + second, first - second
        return [[o[:, :points] for o in out], [o[:, points:] for o in out]]

    both = range(2)
    phase = [split(load(0, level)) for level in both]
    spread = [across(phase[level], 0) for level in both]
    slope = [across(phase[level], 1) for level in both]
    value = ahead_both(spread, 0)
    rise = [split(load(1, level)) for level in both]
    grad_x = ahead_both(spread, 1)
    rise = [across(rise[level], 0) for level in both]
    grad_z = ahead_both(slope, 0)
    bend = [split(load(2, level)) for level in both]
    grad_y = ahead_both(rise, 0)
    bend = [across(bend[level], 0) for level in both]
    lap = ahead_both(bend, 0)

    def back(value, at):
        folded = value[0] + value[1], value[0] - value[1]
        return split(
            jnp.concatenate(
                [dot3_left(pair(stream_ref.at[4 + 2 * at + parity]), split(folded[parity])) for parity in range(2)],
                axis=0,
            )
        )

    def put(field, level, modes):
        even, odd = modes[:half], modes[half:]
        for n in range(0, narrow, 2):
            here = slice(n * 64, n * 64 + 128)
            first, second = even[:, here], odd[:, here]
            for own, value in (
                (n, jnp.where(lower, first, pltpu.roll(second, 64, 1))),
                (n + 1, jnp.where(lower, pltpu.roll(first, 64, 1), second)),
            ):
                for block in range(4):
                    sent[rows(own, field, block, level), :] = value[block * wide : (block + 1) * wide]

    cubed = [[v * v * v for v in value[level]] for level in both]
    explicit = [
        [c - (1.0 + stabilize) * v for c, v in zip(cubed[level], value[level])] for level in both
    ]
    explicit = [back(explicit[level], 0) for level in both]
    push = [
        [capillary * (c - v - interface_sq * l) for c, v, l in zip(cubed[level], value[level], lap[level])]
        for level in both
    ]

    def force(level, slopes):
        return [p * g for p, g in zip(push[level], slopes[level])]

    along = [back(force(level, grad_y), 0) for level in both]
    for level in both:
        put(0, level, dot3(explicit[level], pair(span_ref.at[0])))
    spread = [back(force(level, grad_x), 1) for level in both]
    for level in both:
        put(1, level, dot3(along[level], pair(span_ref.at[0])))
    slope = [back(force(level, grad_z), 0) for level in both]
    for level in both:
        put(2, level, dot3(spread[level], pair(span_ref.at[0])) + dot3(slope[level], pair(span_ref.at[2])))


def update_kernel(
    sizes,
    recv_ref,
    eig_ref,
    velocity_ref,
    dual_ref,
    slope_ref,
    basis_ref,
    decay_ref,
    phase_out,
    velocity_out,
    phase_ref,
    result_ref,
    sems,
):
    half = eig_ref.shape[0] // 2
    width = 256
    columns = range(0, eig_ref.shape[1], width)

    def get(field, column):
        rows = flat_rows(recv_ref)
        return jnp.concatenate(
            [
                jnp.concatenate(
                    [
                        rows[pl.ds(field * 8 + (column // 128 + block) * 2 + level, half, stride=24), :]
                        for block in range(width // 128)
                    ],
                    axis=1,
                )
                for level in range(2)
            ],
            axis=0,
        )

    dual = split(dual_ref[...])
    slope = split(slope_ref[...])
    basis = split(basis_ref[...])
    decay = upright(decay_ref, width)
    waves = [wave_squared(column, width, *sizes) for column in columns]
    operators = [-(decay + wave) for wave in waves]
    done = []

    def leave(which, column, value):
        ref, out = ((phase_ref, phase_out), (result_ref, velocity_out))[which]
        here = slice(column, column + width)
        ref[here, :] = value
        done.append(pltpu.make_async_copy(ref.at[here], out.at[here], sems.at[len(done)]))
        done[-1].start()

    def new_phase(column, operator, explicit):
        damping = 1.0 + time_step * mobility * -operator * (stabilize + interface_sq * -operator)
        return (eig_ref[:, column : column + width] + time_step * mobility * operator * explicit) / damping

    def new_velocity(operator, speed, forcing):
        return (operator * speed + time_step * forcing) / (operator * (1.0 - time_step * viscosity * operator))

    forcing = [dot3_left(slope, split(get(2, column))) for column in columns]
    explicit = [dot3_left(dual, split(get(0, column))) for column in columns]
    forcing = [split(-wave * get(1, column) - value) for column, wave, value in zip(columns, waves, forcing)]
    explicit = [split(new_phase(*at)) for at in zip(columns, operators, explicit)]
    forcing = [dot3_left(dual, value) for value in forcing]
    turned = split(basis_ref[...].T)
    explicit = [tuple(v.T for v in value) for value in explicit]
    speed = [dot3_left(dual, split(velocity_ref[column : column + width, :].T)) for column in columns]
    for column, value in zip(columns, explicit):
        leave(0, column, dot3(value, turned))
    speed = [split(new_velocity(*at)) for at in zip(operators, speed, forcing)]
    for column, value in zip(columns, speed):
        leave(1, column, dot3(tuple(v.T for v in value), turned))
    for copy in done:
        copy.wait()


hbm = pl.BlockSpec(memory_space=pltpu.HBM)
vmem = pl.BlockSpec(memory_space=pltpu.VMEM)


def call(kernel, ins, outs, shapes, scratch, flops, limit):
    return pl.pallas_call(
        kernel,
        out_shape=shapes,
        in_specs=ins,
        out_specs=outs,
        scratch_shapes=scratch,
        compiler_params=pltpu.CompilerParams(vmem_limit_bytes=limit << 20),
        cost_estimate=pl.CostEstimate(flops=flops, bytes_accessed=4 << 20, transcendentals=0),
    )


def stages(rows_x, rows_z, levels, wide, narrow):
    full_x, full_z = rows_x * wide, rows_z * narrow
    count = rows_x * rows_z
    sizes = rows_x, rows_z, full_x, full_z
    square = jax.ShapeDtypeStruct((levels, count), f32)
    result = jax.ShapeDtypeStruct((count, levels), f32)
    parts = jax.ShapeDtypeStruct((wide * narrow, 24, 128), f32)
    buffer = pltpu.VMEM((3, wide * narrow, 8, 128), f32)
    held, line = pltpu.VMEM((levels, count), f32), pltpu.VMEM((1, levels), f32)
    sems = pltpu.SemaphoreType.DMA
    first = call(
        functools.partial(eigen_kernel, sizes),
        [hbm] * 5,
        [hbm] * 2,
        [parts, square],
        [buffer] + [held] * 4 + [line, held, sems((11,))],
        3 * 6 * 512**3,
        60,
    )
    span, stream = (jnp.asarray(t) for t in (span_tables(full_z), stream_tables(full_x, wide)))
    planes = call(
        functools.partial(plane_kernel, wide, narrow), [vmem] * 3, vmem, parts, [], 204 * 2 * 256**3, 40
    )
    last = call(
        functools.partial(update_kernel, sizes),
        [vmem] * 7,
        [hbm] * 2,
        [result] * 2,
        [held, held, sems((4,))],
        5 * 6 * 512**3,
        40,
    )
    return first, lambda recv: planes(recv, span, stream), last


def body(phase, velocity, basis, dual_basis, wall_slope, decay_rates):
    rows_x, rows_z, levels = phase.shape
    wide, narrow = lax.axis_size("wide"), lax.axis_size("narrow")
    first, planes, last = stages(rows_x, rows_z, levels, wide, narrow)
    decay = decay_rates.reshape(1, levels)

    def exchange(parts):
        return lax.all_to_all(parts, ("narrow", "wide"), split_axis=0, concat_axis=0, tiled=True)

    send, phase_eig = first(phase.reshape(-1, levels), dual_basis, wall_slope, basis, decay)
    recv = exchange(planes(exchange(send)))
    outs = last(recv, phase_eig, velocity.reshape(-1, levels), dual_basis, wall_slope, basis, decay)
    return tuple(out.reshape(phase.shape) for out in outs)


def solution(mesh):
    return jax.shard_map(
        body,
        mesh=mesh,
        in_specs=(P("wide", "narrow", None), P("wide", "narrow", None), P(), P(), P(), P()),
        out_specs=(P("wide", "narrow", None), P("wide", "narrow", None)),
        check_vma=False,
    )
```

```python
import functools
import math

import jax
import jax.numpy as jnp
import ml_dtypes
import numpy as np
from jax import lax
from jax.experimental import pallas as pl
from jax.experimental.pallas import tpu as pltpu
from jax.sharding import PartitionSpec as P

time_step = 0.1
mobility = 0.5
stabilize = 1.0
interface_sq = 0.25
capillary = 0.5
viscosity = 0.3

f32 = jnp.float32
bf16 = jnp.bfloat16


def wavenumber(length):
    indices = np.arange(length)
    return np.where(indices < length // 2, indices, indices - length) * (2.0 / length)


def tables(length):
    indices = np.arange(length)
    angles = (indices[:, None] * indices[None, :] % length) * (2.0 * math.pi / length)
    scaling = 1.0 / math.sqrt(length)
    cas_table = (np.cos(angles) + np.sin(angles)) * scaling
    slope_table = wavenumber(length)[None, :] * (np.cos(angles) - np.sin(angles)) * scaling
    return cas_table, slope_table


def halves(table):
    high = table.astype(np.float32).astype(ml_dtypes.bfloat16)
    low = (table - high.astype(np.float64)).astype(np.float32).astype(ml_dtypes.bfloat16)
    return np.stack([high, low])


def span_tables(length):
    cas, slope = tables(length)
    return np.stack([halves(cas.T), halves(slope.T), halves(-slope)])


def stream_tables(length, wide):
    cas, slope = tables(length)
    half = length // 2
    order = np.arange(half).reshape(wide, half // wide).T.reshape(half)
    ahead = [table[:half, parity::2][:, order] for table in (cas, slope) for parity in range(2)]
    back = [table[parity::2, :half][order] for table in (cas, -slope.T) for parity in range(2)]
    return np.stack([halves(t) for t in ahead + back])


def split(value):
    high = value.astype(bf16)
    return high, (value - high.astype(f32)).astype(bf16)


def dot3(left, right):
    def dot(a, b):
        return jnp.dot(a, b, preferred_element_type=f32)

    return dot(left[0], right[0]) + (dot(left[0], right[1]) + dot(left[1], right[0]))


def dot3_left(left, right):
    rows = left[0].shape[0]
    first = jnp.dot(jnp.concatenate([left[0], left[1]], axis=0), right[0], preferred_element_type=f32)
    return first[:rows] + first[rows:] + jnp.dot(left[0], right[1], preferred_element_type=f32)


def wave_squared(column, width, rows_x, rows_z, full_x, full_z):
    at = lax.broadcasted_iota(jnp.int32, (1, width), 1) + column

    def squared(first, own, length):
        index = first + own
        signed = jnp.where(index < length // 2, index, index - length)
        return (signed.astype(f32) * (2.0 / length)) ** 2

    return squared(lax.axis_index("wide") * rows_x, at // rows_z, full_x) + squared(
        lax.axis_index("narrow") * rows_z, at % rows_z, full_z
    )


def upright(decay_ref, width):
    turned = jnp.broadcast_to(decay_ref[...], (128, decay_ref.shape[1])).T
    return jnp.concatenate([turned] * (width // 128), axis=1)


def fetch(sources, targets, sems, early):
    copies = [pltpu.make_async_copy(s, t, sems.at[at]) for at, (s, t) in enumerate(zip(sources, targets))]
    for copy in copies[:early]:
        copy.start()
    return copies


def field_rows(ref, field):
    held = ref.at[field]
    return held.reshape(held.shape[0] * held.shape[1], held.shape[2])


def flat_rows(ref):
    return ref.reshape(ref.shape[0] * ref.shape[1], ref.shape[2])


def of_field(ref, field):
    return ref.at[:, field * 8 : field * 8 + 8]


def eigen_kernel(
    sizes, phase_in, dual_in, slope_in, basis_in, decay_in, send_out, eig_out, *scratch
):
    send_ref, phase_ref, dual_ref, slope_ref, basis_ref, decay_ref, eig_ref, sems = scratch
    levels = phase_ref.shape[1]
    half = levels // 2
    width = 256
    columns = range(0, phase_ref.shape[0], width)
    first, second = (pl.ds(column, width) for column in columns)
    copies = fetch(
        [phase_in.at[first], phase_in.at[second], dual_in, slope_in, basis_in, decay_in],
        [phase_ref.at[first], phase_ref.at[second], dual_ref, slope_ref, basis_ref, decay_ref],
        sems,
        4,
    )
    done = []

    def leave(source, target):
        done.append(pltpu.make_async_copy(source, target, sems.at[6 + len(done)]))
        done[-1].start()

    def put(field, values):
        rows = field_rows(send_ref, field)
        for column, value in zip(columns, values):
            for block in range(width // 128):
                for level in range(2):
                    row = (column // 128 + block) * 2 + level
                    rows[pl.ds(row, half, stride=8), :] = value[
                        level * half : (level + 1) * half, block * 128 : (block + 1) * 128
                    ]
        leave(send_ref.at[field], of_field(send_out, field))

    turned = []
    for at, column in enumerate(columns):
        copies[at].wait()
        if at == 0:
            for copy in copies[4:]:
                copy.start()
        turned.append(phase_ref[column : column + width, :].T)
    put(0, turned)
    pairs = [split(value) for value in turned]
    copies[2].wait()
    dual = split(dual_ref[...])
    eig = [dot3_left(dual, pair) for pair in pairs]
    for column, value in zip(columns, eig):
        eig_ref[:, column : column + width] = value
    leave(eig_ref, eig_out)
    copies[3].wait()
    slope = split(slope_ref[...])
    put(1, [dot3_left(slope, pair) for pair in pairs])
    copies[4].wait()
    copies[5].wait()
    basis = split(basis_ref[...])
    decay = upright(decay_ref, width)
    scaled = [
        split(-(decay + wave_squared(column, width, *sizes)) * value) for column, value in zip(columns, eig)
    ]
    rows = field_rows(send_ref, 2)
    part = half // 2
    for own in range(2):
        mine = [
            jnp.concatenate([b[at : at + part] for at in (own * part, half + own * part)], axis=0) for b in basis
        ]
        for column, pair in zip(columns, scaled):
            value = dot3_left(mine, pair)
            for block in range(width // 128):
                for level in range(2):
                    row = own * part * 8 + (column // 128 + block) * 2 + level
                    rows[pl.ds(row, part, stride=8), :] = value[
                        level * part : (level + 1) * part, block * 128 : (block + 1) * 128
                    ]
        devices = slice(own * part, (own + 1) * part)
        leave(send_ref.at[2, devices], send_out.at[devices, 16:24])
    for copy in done:
        copy.wait()


def plane_kernel(wide, narrow, recv_ref, span_ref, stream_ref, send_ref):
    received, sent = flat_rows(recv_ref), flat_rows(send_ref)

    def pair(ref):
        return ref[0], ref[1]

    lower = lax.broadcasted_iota(jnp.int32, (4 * wide, 128), 1) < 64

    def rows(n, field, block, level):
        return pl.ds(n * wide * 24 + field * 8 + block * 2 + level, wide, stride=24)

    def load(field, level):
        parts = [
            jnp.concatenate([received[rows(n, field, block, level), :] for block in range(4)], axis=0)
            for n in range(narrow)
        ]
        turned = [pltpu.roll(part, 64, 1) for part in parts]
        even = [jnp.where(lower, parts[n], turned[n + 1]) for n in range(0, narrow, 2)]
        odd = [jnp.where(lower, turned[n], parts[n + 1]) for n in range(0, narrow, 2)]
        return jnp.concatenate([jnp.concatenate(even, axis=1), jnp.concatenate(odd, axis=1)], axis=0)

    half = 4 * wide

    def across(values, at):
        return split(dot3_left(values, pair(span_ref.at[at])))

    def ahead(field, at):
        first = dot3_left(pair(stream_ref.at[2 * at]), tuple(f[:half] for f in field))
        second = dot3_left(pair(stream_ref.at[2 * at + 1]), tuple(f[half:] for f in field))
        return first + second, first - second

    def beside(pairs):
        return tuple(jnp.concatenate(part, axis=1) for part in zip(*pairs))

    def ahead_both(fields, at):
        first = dot3_left(pair(stream_ref.at[2 * at]), beside([tuple(f[:half] for f in field) for field in fields]))
        second = dot3_left(
            pair(stream_ref.at[2 * at + 1]), beside([tuple(f[half:] for f in field) for field in fields])
        )
        points = first.shape[1] // 2
        out = first + second, first - second
        return [[o[:, :points] for o in out], [o[:, points:] for o in out]]

    both = range(2)
    phase = [split(load(0, level)) for level in both]
    spread = [across(phase[level], 0) for level in both]
    slope = [across(phase[level], 1) for level in both]
    value = ahead_both(spread, 0)
    rise = [split(load(1, level)) for level in both]
    grad_x = ahead_both(spread, 1)
    rise = [across(rise[level], 0) for level in both]
    grad_z = ahead_both(slope, 0)
    bend = [split(load(2, level)) for level in both]
    grad_y = ahead_both(rise, 0)
    bend = [across(bend[level], 0) for level in both]
    lap = ahead_both(bend, 0)

    def back(value, at):
        folded = value[0] + value[1], value[0] - value[1]
        return split(
            jnp.concatenate(
                [dot3_left(pair(stream_ref.at[4 + 2 * at + parity]), split(folded[parity])) for parity in range(2)],
                axis=0,
            )
        )

    def put(field, level, modes):
        even, odd = modes[:half], modes[half:]
        for n in range(0, narrow, 2):
            here = slice(n * 64, n * 64 + 128)
            first, second = even[:, here], odd[:, here]
            for own, value in (
                (n, jnp.where(lower, first, pltpu.roll(second, 64, 1))),
                (n + 1, jnp.where(lower, pltpu.roll(first, 64, 1), second)),
            ):
                for block in range(4):
                    sent[rows(own, field, block, level), :] = value[block * wide : (block + 1) * wide]

    cubed = [[v * v * v for v in value[level]] for level in both]
    explicit = [
        [c - (1.0 + stabilize) * v for c, v in zip(cubed[level], value[level])] for level in both
    ]
    explicit = [back(explicit[level], 0) for level in both]
    push = [
        [capillary * (c - v - interface_sq * l) for c, v, l in zip(cubed[level], value[level], lap[level])]
        for level in both
    ]

    def force(level, slopes):
        return [p * g for p, g in zip(push[level], slopes[level])]

    along = [back(force(level, grad_y), 0) for level in both]
    for level in both:
        put(0, level, dot3(explicit[level], pair(span_ref.at[0])))
    spread = [back(force(level, grad_x), 1) for level in both]
    for level in both:
        put(1, level, dot3(along[level], pair(span_ref.at[0])))
    slope = [back(force(level, grad_z), 0) for level in both]
    for level in both:
        put(2, level, dot3(spread[level], pair(span_ref.at[0])) + dot3(slope[level], pair(span_ref.at[2])))


def update_kernel(
    sizes,
    recv_ref,
    eig_ref,
    velocity_ref,
    dual_ref,
    slope_ref,
    basis_ref,
    decay_ref,
    phase_out,
    velocity_out,
    phase_ref,
    result_ref,
    sems,
):
    half = eig_ref.shape[0] // 2
    width = 256
    columns = range(0, eig_ref.shape[1], width)

    def get(field, column):
        rows = flat_rows(recv_ref)
        return jnp.concatenate(
            [
                jnp.concatenate(
                    [
                        rows[pl.ds(field * 8 + (column // 128 + block) * 2 + level, half, stride=24), :]
                        for block in range(width // 128)
                    ],
                    axis=1,
                )
                for level in range(2)
            ],
            axis=0,
        )

    dual = split(dual_ref[...])
    slope = split(slope_ref[...])
    basis = split(basis_ref[...])
    decay = upright(decay_ref, width)
    waves = [wave_squared(column, width, *sizes) for column in columns]
    operators = [-(decay + wave) for wave in waves]
    done = []

    def leave(which, column, value):
        ref, out = ((phase_ref, phase_out), (result_ref, velocity_out))[which]
        here = slice(column, column + value.shape[0])
        ref[here, :] = value
        done.append(pltpu.make_async_copy(ref.at[here], out.at[here], sems.at[len(done)]))
        done[-1].start()

    def new_phase(column, operator, explicit):
        damping = 1.0 + time_step * mobility * -operator * (stabilize + interface_sq * -operator)
        return (eig_ref[:, column : column + width] + time_step * mobility * operator * explicit) / damping

    def new_velocity(operator, speed, forcing):
        return (operator * speed + time_step * forcing) / (operator * (1.0 - time_step * viscosity * operator))

    forcing = [dot3_left(slope, split(get(2, column))) for column in columns]
    explicit = [dot3_left(dual, split(get(0, column))) for column in columns]
    forcing = [split(-wave * get(1, column) - value) for column, wave, value in zip(columns, waves, forcing)]
    explicit = [split(new_phase(*at)) for at in zip(columns, operators, explicit)]
    forcing = [dot3_left(dual, value) for value in forcing]
    turned = split(basis_ref[...].T)
    explicit = [tuple(v.T for v in value) for value in explicit]
    speed = [dot3_left(dual, split(velocity_ref[column : column + width, :].T)) for column in columns]
    for column, value in zip(columns, explicit):
        leave(0, column, dot3(value, turned))
    speed = [split(new_velocity(*at)) for at in zip(operators, speed, forcing)]
    for column, value in zip(columns, speed):
        value = tuple(v.T for v in value)
        for part in range(0, width, 128):
            leave(1, column + part, dot3(tuple(v[part : part + 128] for v in value), turned))
    for copy in done:
        copy.wait()


hbm = pl.BlockSpec(memory_space=pltpu.HBM)
vmem = pl.BlockSpec(memory_space=pltpu.VMEM)


def call(kernel, ins, outs, shapes, scratch, flops, limit):
    return pl.pallas_call(
        kernel,
        out_shape=shapes,
        in_specs=ins,
        out_specs=outs,
        scratch_shapes=scratch,
        compiler_params=pltpu.CompilerParams(vmem_limit_bytes=limit << 20),
        cost_estimate=pl.CostEstimate(flops=flops, bytes_accessed=4 << 20, transcendentals=0),
    )


def stages(rows_x, rows_z, levels, wide, narrow):
    full_x, full_z = rows_x * wide, rows_z * narrow
    count = rows_x * rows_z
    sizes = rows_x, rows_z, full_x, full_z
    square = jax.ShapeDtypeStruct((levels, count), f32)
    result = jax.ShapeDtypeStruct((count, levels), f32)
    parts = jax.ShapeDtypeStruct((wide * narrow, 24, 128), f32)
    buffer = pltpu.VMEM((3, wide * narrow, 8, 128), f32)
    held, line = pltpu.VMEM((levels, count), f32), pltpu.VMEM((1, levels), f32)
    sems = pltpu.SemaphoreType.DMA
    first = call(
        functools.partial(eigen_kernel, sizes),
        [hbm] * 5,
        [hbm] * 2,
        [parts, square],
        [buffer] + [held] * 4 + [line, held, sems((11,))],
        3 * 6 * 512**3,
        60,
    )
    span, stream = (jnp.asarray(t) for t in (span_tables(full_z), stream_tables(full_x, wide)))
    planes = call(
        functools.partial(plane_kernel, wide, narrow), [vmem] * 3, vmem, parts, [], 204 * 2 * 256**3, 40
    )
    last = call(
        functools.partial(update_kernel, sizes),
        [vmem] * 7,
        [hbm] * 2,
        [result] * 2,
        [held, held, sems((6,))],
        5 * 6 * 512**3,
        40,
    )
    return first, lambda recv: planes(recv, span, stream), last


def body(phase, velocity, basis, dual_basis, wall_slope, decay_rates):
    rows_x, rows_z, levels = phase.shape
    wide, narrow = lax.axis_size("wide"), lax.axis_size("narrow")
    first, planes, last = stages(rows_x, rows_z, levels, wide, narrow)
    decay = decay_rates.reshape(1, levels)

    def exchange(parts):
        return lax.all_to_all(parts, ("narrow", "wide"), split_axis=0, concat_axis=0, tiled=True)

    send, phase_eig = first(phase.reshape(-1, levels), dual_basis, wall_slope, basis, decay)
    recv = exchange(planes(exchange(send)))
    outs = last(recv, phase_eig, velocity.reshape(-1, levels), dual_basis, wall_slope, basis, decay)
    return tuple(out.reshape(phase.shape) for out in outs)


def solution(mesh):
    return jax.shard_map(
        body,
        mesh=mesh,
        in_specs=(P("wide", "narrow", None), P("wide", "narrow", None), P(), P(), P(), P()),
        out_specs=(P("wide", "narrow", None), P("wide", "narrow", None)),
        check_vma=False,
    )
```

```python
import functools
import math

import jax
import jax.numpy as jnp
import ml_dtypes
import numpy as np
from jax import lax
from jax.experimental import pallas as pl
from jax.experimental.pallas import tpu as pltpu
from jax.sharding import PartitionSpec as P

time_step = 0.1
mobility = 0.5
stabilize = 1.0
interface_sq = 0.25
capillary = 0.5
viscosity = 0.3

f32 = jnp.float32
bf16 = jnp.bfloat16


def wavenumber(length):
    indices = np.arange(length)
    return np.where(indices < length // 2, indices, indices - length) * (2.0 / length)


def tables(length):
    indices = np.arange(length)
    angles = (indices[:, None] * indices[None, :] % length) * (2.0 * math.pi / length)
    scaling = 1.0 / math.sqrt(length)
    cas_table = (np.cos(angles) + np.sin(angles)) * scaling
    slope_table = wavenumber(length)[None, :] * (np.cos(angles) - np.sin(angles)) * scaling
    return cas_table, slope_table


def halves(table):
    high = table.astype(np.float32).astype(ml_dtypes.bfloat16)
    low = (table - high.astype(np.float64)).astype(np.float32).astype(ml_dtypes.bfloat16)
    return np.stack([high, low])


def span_tables(length):
    cas, slope = tables(length)
    return np.stack([halves(cas.T), halves(slope.T), halves(-slope)])


def stream_tables(length, wide):
    cas, slope = tables(length)
    half = length // 2
    order = np.arange(half).reshape(wide, half // wide).T.reshape(half)
    ahead = [table[:half, parity::2][:, order] for table in (cas, slope) for parity in range(2)]
    back = [table[parity::2, :half][order] for table in (cas, -slope.T) for parity in range(2)]
    return np.stack([halves(t) for t in ahead + back])


def split(value):
    high = value.astype(bf16)
    return high, (value - high.astype(f32)).astype(bf16)


def dot3(left, right):
    def dot(a, b):
        return jnp.dot(a, b, preferred_element_type=f32)

    return dot(left[0], right[0]) + (dot(left[0], right[1]) + dot(left[1], right[0]))


def dot3_left(left, right):
    rows = left[0].shape[0]
    first = jnp.dot(jnp.concatenate([left[0], left[1]], axis=0), right[0], preferred_element_type=f32)
    return first[:rows] + first[rows:] + jnp.dot(left[0], right[1], preferred_element_type=f32)


def wave_squared(column, width, rows_x, rows_z, full_x, full_z):
    at = lax.broadcasted_iota(jnp.int32, (1, width), 1) + column

    def squared(first, own, length):
        index = first + own
        signed = jnp.where(index < length // 2, index, index - length)
        return (signed.astype(f32) * (2.0 / length)) ** 2

    return squared(lax.axis_index("wide") * rows_x, at // rows_z, full_x) + squared(
        lax.axis_index("narrow") * rows_z, at % rows_z, full_z
    )


def upright(decay_ref, width):
    turned = jnp.broadcast_to(decay_ref[...], (128, decay_ref.shape[1])).T
    return jnp.concatenate([turned] * (width // 128), axis=1)


def fetch(sources, targets, sems, early):
    copies = [pltpu.make_async_copy(s, t, sems.at[at]) for at, (s, t) in enumerate(zip(sources, targets))]
    for copy in copies[:early]:
        copy.start()
    return copies


def field_rows(ref, field):
    held = ref.at[field]
    return held.reshape(held.shape[0] * held.shape[1], held.shape[2])


def flat_rows(ref):
    return ref.reshape(ref.shape[0] * ref.shape[1], ref.shape[2])


def of_field(ref, field):
    return ref.at[:, field * 8 : field * 8 + 8]


def eigen_kernel(
    sizes, phase_in, dual_in, slope_in, basis_in, decay_in, send_out, eig_out, *scratch
):
    send_ref, phase_ref, dual_ref, slope_ref, basis_ref, decay_ref, eig_ref, sems = scratch
    levels = phase_ref.shape[1]
    half = levels // 2
    width = 256
    columns = range(0, phase_ref.shape[0], width)
    first, second = (pl.ds(column, width) for column in columns)
    copies = fetch(
        [phase_in.at[first], phase_in.at[second], dual_in, slope_in, basis_in, decay_in],
        [phase_ref.at[first], phase_ref.at[second], dual_ref, slope_ref, basis_ref, decay_ref],
        sems,
        4,
    )
    done = []

    def leave(source, target):
        done.append(pltpu.make_async_copy(source, target, sems.at[6 + len(done)]))
        done[-1].start()

    def put(field, values):
        rows = field_rows(send_ref, field)
        for column, value in zip(columns, values):
            for block in range(width // 128):
                for level in range(2):
                    row = (column // 128 + block) * 2 + level
                    rows[pl.ds(row, half, stride=8), :] = value[
                        level * half : (level + 1) * half, block * 128 : (block + 1) * 128
                    ]
        leave(send_ref.at[field], of_field(send_out, field))

    turned = []
    for at, column in enumerate(columns):
        copies[at].wait()
        if at == 0:
            for copy in copies[4:]:
                copy.start()
        turned.append(phase_ref[column : column + width, :].T)
    put(0, turned)
    pairs = [split(value) for value in turned]
    copies[2].wait()
    dual = split(dual_ref[...])
    eig = [dot3_left(dual, pair) for pair in pairs]
    for column, value in zip(columns, eig):
        eig_ref[:, column : column + width] = value
    copies[3].wait()
    slope = split(slope_ref[...])
    put(1, [dot3_left(slope, pair) for pair in pairs])
    leave(eig_ref, eig_out)
    copies[4].wait()
    copies[5].wait()
    basis = split(basis_ref[...])
    decay = upright(decay_ref, width)
    scaled = [
        split(-(decay + wave_squared(column, width, *sizes)) * value) for column, value in zip(columns, eig)
    ]
    rows = field_rows(send_ref, 2)
    part = half // 2
    for own in range(2):
        mine = [
            jnp.concatenate([b[at : at + part] for at in (own * part, half + own * part)], axis=0) for b in basis
        ]
        for column, pair in zip(columns, scaled):
            value = dot3_left(mine, pair)
            for block in range(width // 128):
                for level in range(2):
                    row = own * part * 8 + (column // 128 + block) * 2 + level
                    rows[pl.ds(row, part, stride=8), :] = value[
                        level * part : (level + 1) * part, block * 128 : (block + 1) * 128
                    ]
        devices = slice(own * part, (own + 1) * part)
        leave(send_ref.at[2, devices], send_out.at[devices, 16:24])
    for copy in done:
        copy.wait()


def plane_kernel(wide, narrow, recv_ref, span_ref, stream_ref, send_ref):
    received, sent = flat_rows(recv_ref), flat_rows(send_ref)

    def pair(ref):
        return ref[0], ref[1]

    lower = lax.broadcasted_iota(jnp.int32, (4 * wide, 128), 1) < 64

    def rows(n, field, block, level):
        return pl.ds(n * wide * 24 + field * 8 + block * 2 + level, wide, stride=24)

    def load(field, level):
        parts = [
            jnp.concatenate([received[rows(n, field, block, level), :] for block in range(4)], axis=0)
            for n in range(narrow)
        ]
        turned = [pltpu.roll(part, 64, 1) for part in parts]
        even = [jnp.where(lower, parts[n], turned[n + 1]) for n in range(0, narrow, 2)]
        odd = [jnp.where(lower, turned[n], parts[n + 1]) for n in range(0, narrow, 2)]
        return jnp.concatenate([jnp.concatenate(even, axis=1), jnp.concatenate(odd, axis=1)], axis=0)

    half = 4 * wide

    def across(values, at):
        return split(dot3_left(values, pair(span_ref.at[at])))

    def ahead(field, at):
        first = dot3_left(pair(stream_ref.at[2 * at]), tuple(f[:half] for f in field))
        second = dot3_left(pair(stream_ref.at[2 * at + 1]), tuple(f[half:] for f in field))
        return first + second, first - second

    def beside(pairs):
        return tuple(jnp.concatenate(part, axis=1) for part in zip(*pairs))

    def ahead_both(fields, at):
        first = dot3_left(pair(stream_ref.at[2 * at]), beside([tuple(f[:half] for f in field) for field in fields]))
        second = dot3_left(
            pair(stream_ref.at[2 * at + 1]), beside([tuple(f[half:] for f in field) for field in fields])
        )
        points = first.shape[1] // 2
        out = first + second, first - second
        return [[o[:, :points] for o in out], [o[:, points:] for o in out]]

    both = range(2)
    phase = [split(load(0, level)) for level in both]
    spread = [across(phase[level], 0) for level in both]
    slope = [across(phase[level], 1) for level in both]
    value = ahead_both(spread, 0)
    rise = [split(load(1, level)) for level in both]
    grad_x = ahead_both(spread, 1)
    rise = [across(rise[level], 0) for level in both]
    grad_z = ahead_both(slope, 0)
    bend = [split(load(2, level)) for level in both]
    grad_y = ahead_both(rise, 0)
    bend = [across(bend[level], 0) for level in both]
    lap = ahead_both(bend, 0)

    def back(value, at):
        folded = value[0] + value[1], value[0] - value[1]
        return split(
            jnp.concatenate(
                [dot3_left(pair(stream_ref.at[4 + 2 * at + parity]), split(folded[parity])) for parity in range(2)],
                axis=0,
            )
        )

    def put(field, level, modes):
        even, odd = modes[:half], modes[half:]
        for n in range(0, narrow, 2):
            here = slice(n * 64, n * 64 + 128)
            first, second = even[:, here], odd[:, here]
            for own, value in (
                (n, jnp.where(lower, first, pltpu.roll(second, 64, 1))),
                (n + 1, jnp.where(lower, pltpu.roll(first, 64, 1), second)),
            ):
                for block in range(4):
                    sent[rows(own, field, block, level), :] = value[block * wide : (block + 1) * wide]

    cubed = [[v * v * v for v in value[level]] for level in both]
    explicit = [
        [c - (1.0 + stabilize) * v for c, v in zip(cubed[level], value[level])] for level in both
    ]
    explicit = [back(explicit[level], 0) for level in both]
    push = [
        [capillary * (c - v - interface_sq * l) for c, v, l in zip(cubed[level], value[level], lap[level])]
        for level in both
    ]

    def force(level, slopes):
        return [p * g for p, g in zip(push[level], slopes[level])]

    along = [back(force(level, grad_y), 0) for level in both]
    for level in both:
        put(0, level, dot3(explicit[level], pair(span_ref.at[0])))
    spread = [back(force(level, grad_x), 1) for level in both]
    for level in both:
        put(1, level, dot3(along[level], pair(span_ref.at[0])))
    slope = [back(force(level, grad_z), 0) for level in both]
    for level in both:
        put(2, level, dot3(spread[level], pair(span_ref.at[0])) + dot3(slope[level], pair(span_ref.at[2])))


def update_kernel(
    sizes,
    recv_ref,
    eig_ref,
    velocity_ref,
    dual_ref,
    slope_ref,
    basis_ref,
    decay_ref,
    phase_out,
    velocity_out,
    phase_ref,
    result_ref,
    sems,
):
    half = eig_ref.shape[0] // 2
    width = 256
    columns = range(0, eig_ref.shape[1], width)

    def get(field, column):
        rows = flat_rows(recv_ref)
        return jnp.concatenate(
            [
                jnp.concatenate(
                    [
                        rows[pl.ds(field * 8 + (column // 128 + block) * 2 + level, half, stride=24), :]
                        for block in range(width // 128)
                    ],
                    axis=1,
                )
                for level in range(2)
            ],
            axis=0,
        )

    dual = split(dual_ref[...])
    slope = split(slope_ref[...])
    basis = split(basis_ref[...])
    decay = upright(decay_ref, width)
    waves = [wave_squared(column, width, *sizes) for column in columns]
    operators = [-(decay + wave) for wave in waves]
    done = []

    def leave(which, column, value):
        ref, out = ((phase_ref, phase_out), (result_ref, velocity_out))[which]
        here = slice(column, column + value.shape[0])
        ref[here, :] = value
        done.append(pltpu.make_async_copy(ref.at[here], out.at[here], sems.at[len(done)]))
        done[-1].start()

    def new_phase(column, operator, explicit):
        damping = 1.0 + time_step * mobility * -operator * (stabilize + interface_sq * -operator)
        return (eig_ref[:, column : column + width] + time_step * mobility * operator * explicit) / damping

    def new_velocity(operator, speed, forcing):
        return (operator * speed + time_step * forcing) / (operator * (1.0 - time_step * viscosity * operator))

    forcing = [dot3_left(slope, split(get(2, column))) for column in columns]
    explicit = [dot3_left(dual, split(get(0, column))) for column in columns]
    forcing = [split(-wave * get(1, column) - value) for column, wave, value in zip(columns, waves, forcing)]
    explicit = [split(new_phase(*at)) for at in zip(columns, operators, explicit)]
    forcing = [dot3_left(dual, value) for value in forcing]
    turned = split(basis_ref[...].T)
    explicit = [tuple(v.T for v in value) for value in explicit]
    speed = [dot3_left(dual, split(velocity_ref[column : column + width, :].T)) for column in columns]
    for column, value in zip(columns, explicit):
        leave(0, column, dot3(value, turned))
    speed = [split(new_velocity(*at)) for at in zip(operators, speed, forcing)]
    for column, value in zip(columns, speed):
        value = tuple(v.T for v in value)
        for part in range(0, width, 128):
            leave(1, column + part, dot3(tuple(v[part : part + 128] for v in value), turned))
    for copy in done:
        copy.wait()


hbm = pl.BlockSpec(memory_space=pltpu.HBM)
vmem = pl.BlockSpec(memory_space=pltpu.VMEM)


def call(kernel, ins, outs, shapes, scratch, flops, limit):
    return pl.pallas_call(
        kernel,
        out_shape=shapes,
        in_specs=ins,
        out_specs=outs,
        scratch_shapes=scratch,
        compiler_params=pltpu.CompilerParams(vmem_limit_bytes=limit << 20),
        cost_estimate=pl.CostEstimate(flops=flops, bytes_accessed=4 << 20, transcendentals=0),
    )


def stages(rows_x, rows_z, levels, wide, narrow):
    full_x, full_z = rows_x * wide, rows_z * narrow
    count = rows_x * rows_z
    sizes = rows_x, rows_z, full_x, full_z
    square = jax.ShapeDtypeStruct((levels, count), f32)
    result = jax.ShapeDtypeStruct((count, levels), f32)
    parts = jax.ShapeDtypeStruct((wide * narrow, 24, 128), f32)
    buffer = pltpu.VMEM((3, wide * narrow, 8, 128), f32)
    held, line = pltpu.VMEM((levels, count), f32), pltpu.VMEM((1, levels), f32)
    sems = pltpu.SemaphoreType.DMA
    first = call(
        functools.partial(eigen_kernel, sizes),
        [hbm] * 5,
        [hbm] * 2,
        [parts, square],
        [buffer] + [held] * 4 + [line, held, sems((11,))],
        3 * 6 * 512**3,
        60,
    )
    span, stream = (jnp.asarray(t) for t in (span_tables(full_z), stream_tables(full_x, wide)))
    planes = call(
        functools.partial(plane_kernel, wide, narrow), [vmem] * 3, vmem, parts, [], 204 * 2 * 256**3, 40
    )
    last = call(
        functools.partial(update_kernel, sizes),
        [vmem] * 7,
        [hbm] * 2,
        [result] * 2,
        [held, held, sems((6,))],
        5 * 6 * 512**3,
        40,
    )
    return first, lambda recv: planes(recv, span, stream), last


def body(phase, velocity, basis, dual_basis, wall_slope, decay_rates):
    rows_x, rows_z, levels = phase.shape
    wide, narrow = lax.axis_size("wide"), lax.axis_size("narrow")
    first, planes, last = stages(rows_x, rows_z, levels, wide, narrow)
    decay = decay_rates.reshape(1, levels)

    def exchange(parts):
        return lax.all_to_all(parts, ("narrow", "wide"), split_axis=0, concat_axis=0, tiled=True)

    send, phase_eig = first(phase.reshape(-1, levels), dual_basis, wall_slope, basis, decay)
    recv = exchange(planes(exchange(send)))
    outs = last(recv, phase_eig, velocity.reshape(-1, levels), dual_basis, wall_slope, basis, decay)
    return tuple(out.reshape(phase.shape) for out in outs)


def solution(mesh):
    return jax.shard_map(
        body,
        mesh=mesh,
        in_specs=(P("wide", "narrow", None), P("wide", "narrow", None), P(), P(), P(), P()),
        out_specs=(P("wide", "narrow", None), P("wide", "narrow", None)),
        check_vma=False,
    )
```
